32 devices in a mesh: ctx: 8 (over z, x), grp: 4 (over y, core).
Axes of the slice: x: 2, y: 2, z: 4, core: 2. Of those that a mesh axis runs over, the one named last changes fastest.
Arguments:
- out_grad: bfloat16 [4096, 2048], P('ctx', 'grp'), may hold values from -6 to 6
- filter_mats: bfloat16 [16, 2048, 2048], P('grp', 'ctx'), may hold values from -0.125 to 0.125
- coeffs: float32 [16, 80], replicated, may hold values from -0.15625 to 0.15625
- pole_rates: float32 [80], replicated, may hold values from 4.8828124e-06 to 0.03
Outputs:
- in_grad: bfloat16 [4096, 2048], P('ctx', 'grp')
The draws below stay inside these ranges and needn't reach their ends.
All inputs are finite; a program needn't handle non-finite values.
Results may differ from the reference program's by a relative error of at most 0.001.
Values may be sent and summed in bfloat16 or wider, within the bound.
No kernel may reach another device: no remote copies, remote signals or barrier semaphores. Data moves between devices by JAX's collectives and lax.ppermute only.
A program may use at most 128 MiB of HBM per device.

```python
import math
import jax
import jax.numpy as jnp
from jax import lax

D = 2048
K = 16
P_SIZE = 80
TOK_DEV = 512
TOKENS = 4096
N_CTX = 8


def block_scale(rng, extent, cuts, smallest, high):
    loudness, own = 1.0, jax.random.fold_in(rng, 6)
    for axis_at, blocks in cuts:
        steps = jnp.exp(jax.random.uniform(jax.random.fold_in(own, axis_at), (blocks,), jnp.float32, smallest / len(cuts), high / len(cuts)))
        loudness = loudness * jnp.repeat(steps, extent[axis_at] // blocks).reshape([-1 if axis == axis_at else 1 for axis in range(len(extent))])
    return loudness


def bell_draw(rng, extent, spread, most, shards=(), kind=jnp.bfloat16):
    loudness = block_scale(rng, extent, shards, -0.22, 0.18) if shards else 1.0
    values = jax.random.normal(rng, extent, jnp.float32) * spread * loudness
    return jnp.minimum(jnp.maximum(values, -most), most).astype(kind)


def setup_inputs(seed: int = 0) -> dict:
    arg_keys = jax.random.split(jax.random.key(seed), 5)
    return {
        "out_grad": bell_draw(arg_keys[0], (TOKENS, D), 1.0, 6.0, ((0, 8), (1, 4))),
        "filter_mats": bell_draw(arg_keys[1], (K, D, D), D ** -0.5, 0.125, ((0, 4), (1, 8))),
        "coeffs": bell_draw(arg_keys[2], (K, P_SIZE), (K * P_SIZE) ** -0.5, 0.15625, (), jnp.float32),
        "pole_rates": jnp.clip(jnp.exp(jax.random.uniform(arg_keys[3], (P_SIZE,), jnp.float32, math.log(4.882812390860636e-06), math.log(0.03))), 4.882812390860636e-06, 0.03),
    }


def reference(out_grad, filter_mats, coeffs, pole_rates):
    exact_prec = lax.Precision.HIGHEST
    pole_gains = jnp.sqrt(-jnp.expm1(-2.0 * pole_rates))
    positions = jnp.arange(TOK_DEV).astype(jnp.float32)
    lag_mat = positions[:, None] - positions[None, :]
    causal = lag_mat >= 0.0
    lag_pos = jnp.where(causal, lag_mat, jnp.float32(0.0))
    scaled = coeffs * pole_gains[None, :]

    def kernel_one(coef_row):
        values = lax.optimization_barrier(jnp.sum(coef_row[:, None, None] * jnp.exp(-pole_rates[:, None, None] * lag_pos[None]), axis=0))
        return jnp.where(causal, values, jnp.float32(0.0))
    kernel_mat = lax.map(kernel_one, scaled)
    decay_pos = jnp.exp(-positions[:, None] * pole_rates[None, :])
    weights = coeffs[:, :, None] * decay_pos.T[None]
    edge_decay = pole_gains[None, :] * jnp.exp(-(TOK_DEV - positions)[:, None] * pole_rates[None, :])
    block_decay = jnp.exp(-TOK_DEV * pole_rates)[:, None]
    mats_wide = filter_mats.astype(jnp.float32)
    blocks = out_grad.reshape(N_CTX, TOK_DEV, D)

    def advance(carried, grad_block):
        proj_grad = jnp.einsum('tj,kij->kti', grad_block.astype(jnp.float32), mats_wide, precision=exact_prec)
        near_part = jnp.einsum('kts,kti->si', kernel_mat, proj_grad, precision=exact_prec)
        far_part = jnp.dot(edge_decay, carried, precision=exact_prec)
        result = (near_part + far_part).astype(jnp.bfloat16)
        updated = jnp.einsum('kpt,kti->pi', weights, proj_grad, precision=exact_prec) + block_decay * carried
        return (updated, result)
    start_state = jnp.zeros((P_SIZE, D), jnp.float32)
    final_state, results = lax.scan(advance, start_state, blocks, reverse=True)
    return results.reshape(TOKENS, D)
```

```python
import functools

import jax
import jax.numpy as jnp
from jax import lax
from jax.experimental import pallas as pl
from jax.experimental.pallas import tpu as pltpu
from jax.sharding import PartitionSpec as P

exact_prec = lax.Precision.HIGHEST
f32, bf16 = jnp.float32, jnp.bfloat16
NT = (((1,), (1,)), ((), ()))


def split2(x):
    high = x.astype(bf16)
    return high, (x - high.astype(f32)).astype(bf16)


def tables_kernel(rates, coef, scaled, out):
    poles, width = rates.shape[0], out.shape[2] // 4
    lag = lax.broadcasted_iota(jnp.int32, (poles, width), 1).astype(f32)
    decay = jnp.exp(-rates[...] * lag)
    for j in range(2):
        phi = jnp.sum(scaled[j] * decay, axis=0, keepdims=True)
        line = jnp.concatenate([phi, jnp.zeros_like(phi)], axis=1)
        rolled = pltpu.roll(jnp.broadcast_to(line, (width, 2 * width)), 0, 1, stride=1, stride_axis=0)
        for row, part in ((0, rolled[:, :width]), (width, coef[j] * decay)):
            high, low = split2(part)
            rows = pl.ds(row, part.shape[0])
            out[0, rows, j * width : (j + 1) * width] = high
            out[0, rows, (2 + j) * width : (3 + j) * width] = low


def tables(coeffs, rates, gains, width):
    filters, poles = coeffs.shape
    column = pl.BlockSpec((2, poles, 1), lambda i: (i, 0, 0))
    return pl.pallas_call(
        tables_kernel,
        grid=(filters // 2,),
        in_specs=[pl.BlockSpec((poles, 1), lambda i: (0, 0)), column, column],
        out_specs=pl.BlockSpec((1, width + poles, 4 * width), lambda i: (i, 0, 0)),
        out_shape=jax.ShapeDtypeStruct((filters // 2, width + poles, 4 * width), bf16),
        name="pole_tables",
    )(rates[:, None], coeffs[:, :, None], (coeffs * gains[None, :])[:, :, None])


def blocks_kernel(blocks, parts, fresh, info, *refs):
    mine, other = refs[: blocks * parts], refs[blocks * parts : 2 * blocks * parts]
    mats, table = refs[2 * blocks * parts : 2 * blocks * parts + 2]
    rest = refs[2 * blocks * parts + 2 :]
    before, after = ((), rest) if fresh else (rest[:blocks], rest[blocks:])
    wide = mine[0].shape[1]
    here = info[0]
    width = table.shape[2] // 4
    half = mats.shape[1] // 2
    first = pl.program_id(0) == 0
    mats_mine = mats[0, :, pl.ds(pl.multiple_of(here * wide, wide), wide)]
    mats_other = mats[0, :, pl.ds(pl.multiple_of((1 - here) * wide, wide), wide)]
    for b in range(blocks):
        rows_mine = jnp.concatenate([r[...] for r in mine[b * parts : (b + 1) * parts]], axis=0)
        rows_other = jnp.concatenate([r[...] for r in other[b * parts : (b + 1) * parts]], axis=0)
        proj = lax.dot_general(rows_mine, mats_mine, NT, preferred_element_type=f32)
        proj += lax.dot_general(rows_other, mats_other, NT, preferred_element_type=f32)
        high, low = split2(proj)

        def side_by_side(x):
            return [
                jnp.concatenate([x[:width, j * half : (j + 1) * half], x[width:, j * half : (j + 1) * half]], axis=1)
                for j in range(2)
            ]

        h0, h1 = side_by_side(high)
        l0, l1 = side_by_side(low)
        add = jnp.dot(table[0], jnp.concatenate([h0, h1, h0, h1], axis=0), preferred_element_type=f32)
        add += jnp.dot(
            table[0, :, : 2 * width], jnp.concatenate([l0, l1], axis=0), preferred_element_type=f32
        )
        if fresh:
            start = jnp.where(first, 0.0, after[b][...])
        else:
            start = jnp.where(first, before[b][...], after[b][...])
        after[b][...] = start + add


def add_blocks(here, pair_at, mine, other, mats, table, totals):
    blocks, parts = len(mine), len(mine[0])
    assert all(len(m) == parts for m in mine)
    pairs, rows, cols = mats.shape
    height, tw = table.shape[1:]
    fresh = totals is None
    whole = lambda x: pl.BlockSpec(x.shape, lambda i, info: (0,) * x.ndim)
    flat = [p for m in mine for p in m] + [p for m in other for p in m]
    total = jax.ShapeDtypeStruct((height, rows), f32)
    tspec = pl.BlockSpec((height, rows), lambda i, info: (0, 0))
    n = len(flat)
    tokens = sum(p.shape[0] for m in mine for p in m)
    flops = 2 * tokens * pairs * (rows * cols + 2 * 3 * height * rows // 2)
    return pl.pallas_call(
        functools.partial(blocks_kernel, blocks, parts, fresh),
        grid_spec=pltpu.PrefetchScalarGridSpec(
            num_scalar_prefetch=1,
            grid=(pairs,),
            in_specs=[whole(p) for p in flat]
            + [
                pl.BlockSpec((1, rows, cols), lambda i, info: (i, 0, 0)),
                pl.BlockSpec((1, height, tw), lambda i, info: (info[1] + i, 0, 0)),
            ]
            + ([] if fresh else [tspec] * blocks),
            out_specs=[tspec] * blocks,
        ),
        out_shape=[total] * blocks,
        input_output_aliases={} if fresh else {1 + n + 2 + b: b for b in range(blocks)},
        compiler_params=pltpu.CompilerParams(vmem_limit_bytes=48 * 2**20),
        cost_estimate=pl.CostEstimate(
            flops=flops, bytes_accessed=mats.size * 2 + pairs * height * tw * 2 + tokens * cols * 2, transcendentals=0
        ),
        name="add_blocks",
    )(jnp.stack([here, pair_at]).astype(jnp.int32), *flat, mats, table, *([] if fresh else totals))


def finish_kernel(count, info, *refs):
    totals, (edge, decay), out = refs[:count], refs[count : count + 2], refs[count + 2]
    held, sems = refs[count + 3 :]
    for s in range(count):
        pltpu.make_async_copy(totals[s], held.at[info[s]], sems.at[s]).start()
    width, poles = edge.shape
    half = held.shape[2] // 2
    eh, el = split2(edge[...])
    left = jnp.concatenate([eh, el, eh], axis=1)
    for s in range(count):
        pltpu.make_async_copy(totals[s], held.at[info[s]], sems.at[s]).wait()
    per = out.shape[1]
    ways = out.shape[0]
    carried = jnp.zeros((poles, half), f32)
    for c in reversed(range(count)):
        near = held[c, :width, :]
        state = held[c, width:, :]
        inner = state[:, half:] + decay[...] * carried
        entering = jnp.concatenate([inner, carried], axis=1)
        ch, cl = split2(entering)
        far = jnp.dot(left, jnp.concatenate([ch, ch, cl], axis=0), preferred_element_type=f32)
        value = near + far
        way = info[count + 2 * c]
        slot = info[count + 2 * c + 1]
        out[way, slot, :width, :] = value[:, :half]
        out[way, slot, width:, :] = value[:, half:]
        carried = state[:, :half] + decay[...] * inner


def finish(info, totals, edge, decay, ways):
    count = len(totals)
    height, tw = totals[0].shape
    width = edge.shape[0]
    vm = pl.BlockSpec(memory_space=pltpu.VMEM)
    return pl.pallas_call(
        functools.partial(finish_kernel, count),
        grid_spec=pltpu.PrefetchScalarGridSpec(
            num_scalar_prefetch=1,
            grid=(),
            in_specs=[pl.BlockSpec(memory_space=pl.ANY)] * count + [vm, vm],
            out_specs=vm,
            scratch_shapes=[pltpu.VMEM((count, height, tw), f32), pltpu.SemaphoreType.DMA((count,))],
        ),
        out_shape=jax.ShapeDtypeStruct((ways, count // ways, 2 * width, tw // 2), f32),
        compiler_params=pltpu.CompilerParams(vmem_limit_bytes=48 * 2**20),
        name="finish_blocks",
    )(info, *totals, edge, decay)


def plain_tables(coeffs, rates, gains, width):
    lag = jnp.arange(width, dtype=f32)
    decay = jnp.exp(-rates[:, None] * lag[None, :])
    shift = lag[None, :] - lag[:, None]
    phi = jnp.dot(coeffs * gains[None, :], decay, precision=exact_prec)
    near = jnp.where(shift >= 0, phi[:, jnp.maximum(shift, 0).astype(jnp.int32)], 0.0)
    return jnp.concatenate([near, coeffs[:, :, None] * decay[None]], axis=1)


def plain_add(here, pair_at, mine, other, mats, table, totals):
    pairs, rows, cols = mats.shape
    half, wide = rows // 2, cols // 2
    use = lax.dynamic_slice_in_dim(table, 2 * pair_at, 2 * pairs, 0)
    width = table.shape[2]
    swapped = jnp.where(here == 0, mats, jnp.roll(mats, wide, axis=2)).reshape(2 * pairs, half, cols)
    results = []
    for b in range(len(mine)):
        rows_b = jnp.concatenate([jnp.concatenate(mine[b]), jnp.concatenate(other[b])], axis=1)
        proj = jnp.einsum("tj,kij->kti", rows_b, swapped, preferred_element_type=f32)
        proj = jnp.concatenate([proj[:, :width], proj[:, width:]], axis=2)
        add = jnp.einsum("kst,kti->si", use, proj, precision=exact_prec)
        results.append(add if totals is None else totals[b] + add)
    return results


def plain_finish(info, totals, edge, decay, ways):
    count = len(totals)
    width, half = edge.shape[0], totals[0].shape[1] // 2
    held = jnp.zeros((count,) + totals[0].shape, f32)
    out = jnp.zeros((ways, count // ways, 2 * width, half), f32)
    for s in range(count):
        held = lax.dynamic_update_slice(held, totals[s][None], (info[s], 0, 0))
    carried = jnp.zeros((edge.shape[1], half), f32)
    for c in reversed(range(count)):
        near, state = held[c, :width], held[c, width:]
        inner = state[:, half:] + decay * carried
        far = jnp.dot(edge, jnp.concatenate([inner, carried], axis=1), precision=exact_prec)
        value = near + far
        value = jnp.concatenate([value[:, :half], value[:, half:]], axis=0)
        out = lax.dynamic_update_slice(out, value[None, None], (info[count + 2 * c], info[count + 2 * c + 1], 0, 0))
        carried = state[:, :half] + decay * inner
    return out


def per_device(out_grad, filter_mats, coeffs, pole_rates):
    count, groups = lax.axis_size("ctx"), lax.axis_size("grp")
    ctx, grp = lax.axis_index("ctx"), lax.axis_index("grp")
    ways = groups // 2
    way, here = grp // 2, grp % 2
    own_filters, features, _ = filter_mats.shape
    length, wide = out_grad.shape
    half, width = features // 2, length // 2
    kernels = half % 128 == 0 and wide % 128 == 0 and width % 128 == 0 and pole_rates.shape[0] % 16 == 0
    make, add, end = (tables, add_blocks, finish) if kernels else (plain_tables, plain_add, plain_finish)

    def rank(w, h):
        return (w % ways) * 2 + h

    def over_grp(x, by_way, by_core):
        pairs = [(rank(w, h), rank(w + by_way, h ^ by_core)) for w in range(ways) for h in range(2)]
        return lax.ppermute(x, "grp", pairs)

    def piece(by_way, by_core, lo, n):
        to_way, to_core = (way + by_way) % ways, here ^ by_core
        return lax.dynamic_slice(
            filter_mats, (lo, to_core * half, to_way * 2 * wide), (n, half, 2 * wide)
        ).reshape(n // 2, 2 * half, 2 * wide)

    def source_pair(by_way, by_core, lo):
        return (((way - by_way) % ways) * 2 + (here ^ by_core)) * (own_filters // 2) + lo // 2

    far_mats = []
    for lo in range(0, own_filters, 2):
        for by_way in range(1, ways):
            for by_core in (0, 1):
                got = over_grp(piece(by_way, by_core, lo, 2), by_way, by_core)
                far_mats.append((source_pair(by_way, by_core, lo), got))
    near_mats = [
        (source_pair(0, 0, 0), piece(0, 0, 0, own_filters)),
        (source_pair(0, 1, 0), over_grp(piece(0, 1, 0, own_filters), 0, 1)),
    ]

    order = [*range(0, count, 2), *reversed(range(1, count, 2))]
    place = [order.index(c) for c in range(count)]
    right = [(order[i], order[(i + 1) % count]) for i in range(count)]
    left = [(b, a) for a, b in right]
    at = jnp.asarray(place)[ctx]
    order_now = jnp.asarray(order)
    swap = lambda x: over_grp(x, 0, 1)
    own = [out_grad[:width], out_grad[width:]]
    mine, other, holder = [own], [[swap(p) for p in own]], [at]
    going_right, going_left = own, own
    for step in range(1, count // 2 + 1):
        if step < count // 2:
            going_right = [lax.ppermute(p, "ctx", right) for p in going_right]
            going_left = [lax.ppermute(p, "ctx", left) for p in going_left]
            mine += [going_right, going_left]
            other += [[swap(p) for p in going_right], [swap(p) for p in going_left]]
            holder += [(at - step) % count, (at + step) % count]
        else:
            last = [lax.ppermute(going_right[0], "ctx", right), lax.ppermute(going_left[1], "ctx", left)]
            mine.append(last)
            other.append([swap(p) for p in last])
            holder.append((at + step) % count)

    gains = jnp.sqrt(-jnp.expm1(-2.0 * pole_rates))
    table = make(coeffs, pole_rates, gains, width)
    totals = [None] * count

    def run(slots, pair_at, mats):
        have = None if totals[slots[0]] is None else [totals[s] for s in slots]
        got = add(here, pair_at, [mine[s] for s in slots], [other[s] for s in slots], mats, table, have)
        for s, t in zip(slots, got):
            totals[s] = t

    sets = [[0]] + [[s, s + 1] for s in range(1, count - 1, 2)] + [[count - 1]]
    for slots in sets:
        for pair_at, mats in near_mats:
            run(slots, pair_at, mats)
    for pair_at, mats in far_mats:
        for slots in ([*range(count // 2)], [*range(count // 2, count)]):
            run(slots, pair_at, mats)

    per = count // ways
    turn = (ctx % (count // groups)) * 2 + here
    where = [order_now[h] for h in holder]
    for c in range(count):
        where += [(c - ctx - way) % ways, (c // ways - turn) % per]
    step_back = jnp.arange(width, dtype=f32) - width
    edge = gains[None, :] * jnp.exp(step_back[:, None] * pole_rates[None, :])
    decay = jnp.exp(-width * pole_rates)[:, None]
    partial = end(jnp.stack(where).astype(jnp.int32), totals, edge, decay, ways)

    received = []
    for r in range(per):
        total = partial[0, r]
        for by_way in range(1, ways):
            total = total + over_grp(partial[by_way, r], by_way, 0)
        result = total.astype(bf16)
        pairs = []
        for c in range(count):
            for g in range(groups):
                m = (r + (c % (count // groups)) * 2 + g % 2) % per
                to = ways * m + (g // 2 + c) % ways
                pairs.append((c * groups + g, to * groups + c // (count // groups)))
        received.append(lax.ppermute(result, ("ctx", "grp"), pairs))
    stacked = jnp.stack(received)
    picks = (ctx // ways - jnp.arange(per)) % per
    return stacked[picks].transpose(1, 0, 2).reshape(length, wide)


def solution(mesh):
    placed = (P("ctx", "grp"), P("grp", "ctx", None), P(), P())
    return jax.shard_map(
        per_device, mesh=mesh, in_specs=placed, out_specs=P("ctx", "grp"), check_vma=False
    )
```

```python
import functools

import jax
import jax.numpy as jnp
import numpy as np
from jax import lax
from jax.experimental import pallas as pl
from jax.experimental.pallas import tpu as pltpu
from jax.sharding import PartitionSpec as P

exact_prec = lax.Precision.HIGHEST
f32, bf16 = jnp.float32, jnp.bfloat16
NT = (((1,), (1,)), ((), ()))
VM = pl.BlockSpec(memory_space=pltpu.VMEM)
ANY = pl.BlockSpec(memory_space=pl.ANY)
SM = pl.BlockSpec(memory_space=pltpu.SMEM)


def params(mib=16):
    return pltpu.CompilerParams(vmem_limit_bytes=mib * 2**20)


def split2(x):
    high = x.astype(bf16)
    return high, (x - high.astype(f32)).astype(bf16)


def tables_kernel(poles_ref, out):
    poles, height, width = poles_ref.shape[0], out.shape[1], out.shape[2] // 4
    step = width // 2
    rate, gain = poles_ref[:, 0:1], poles_ref[:, 1:2]
    lag = lax.broadcasted_iota(jnp.int32, (poles, width), 1).astype(f32)
    decay = jnp.exp(-rate * lag)
    gained = gain * decay
    columns = lax.broadcasted_iota(jnp.int32, (poles, poles_ref.shape[1]), 1)

    @pl.loop(0, out.shape[0])
    def _(pair):
        for j in range(2):
            chosen = jnp.where(columns == 2 + 2 * pair + j, poles_ref[...], 0.0)
            coef = jnp.sum(chosen, axis=1, keepdims=True)
            phi = jnp.sum(coef * gained, axis=0, keepdims=True)
            line = jnp.concatenate([phi, jnp.zeros((1, step), f32)], axis=1)
            rolled = pltpu.roll(jnp.broadcast_to(line, (step, width + step)), 0, 1, stride=1, stride_axis=0)
            high, low = split2(rolled[:, :width])
            wh, wl = split2(coef * decay)
            for at, near, weight in ((j, high, wh), (2 + j, low, wl)):
                lo = at * width
                out[pair, :step, lo : lo + width] = near
                out[pair, step:width, lo : lo + step] = jnp.zeros((step, step), bf16)
                out[pair, step:width, lo + step : lo + width] = near[:, :step]
                out[pair, width:, lo : lo + width] = weight


def tables(coeffs, rates, gains, width):
    filters, poles = coeffs.shape
    joined = jnp.concatenate([rates[:, None], gains[:, None], coeffs.T], axis=1)
    return pl.pallas_call(
        tables_kernel,
        in_specs=[VM],
        out_specs=VM,
        out_shape=jax.ShapeDtypeStruct((filters // 2, width + poles, 4 * width), bf16),
        compiler_params=params(),
        cost_estimate=pl.CostEstimate(flops=int(4e9), bytes_accessed=0, transcendentals=0),
        name="pole_tables",
    )(joined)


def cut_kernel(plan, info, mats, *refs):
    outs, sems = refs[:-1], refs[-1]
    copies = []
    for i, (lo, n) in enumerate(plan):
        half, cols = outs[i].shape[1:]
        src = mats.at[
            pl.ds(lo, n),
            pl.ds(pl.multiple_of(info[2 * i], half), half),
            pl.ds(pl.multiple_of(info[2 * i + 1], cols), cols),
        ]
        copies.append(pltpu.make_async_copy(src, outs[i], sems.at[i]))
    for c in copies:
        c.start()
    for c in copies:
        c.wait()


def cut(mats, info, plan, half, cols):
    return pl.pallas_call(
        functools.partial(cut_kernel, plan),
        in_specs=[SM, ANY],
        out_specs=[ANY] * len(plan),
        out_shape=[jax.ShapeDtypeStruct((n, half, cols), bf16) for _, n in plan],
        scratch_shapes=[pltpu.SemaphoreType.DMA((len(plan),))],
        compiler_params=params(),
        name="cut_filters",
    )(info, mats)


def blocks_kernel(blocks, sets, fresh, info, *refs):
    mine, other = refs[:blocks], refs[blocks : 2 * blocks]
    mats = refs[2 * blocks : 2 * blocks + sets]
    table = refs[2 * blocks + sets]
    rest = refs[2 * blocks + sets + 1 :]
    before, after, held = rest[:-blocks - 1], rest[-blocks - 1 : -1], rest[-1]
    wide = mine[0].shape[1]
    here = info[0]
    width = table.shape[2] // 4
    half = mats[0].shape[1]
    for b in range(blocks):
        after[b][...] = jnp.zeros_like(after[b]) if fresh else before[b][...]

    @pl.loop(0, mats[0].shape[0] // 2)
    def _(i):
        for n in range(sets):
            two = mats[n].at[pl.ds(2 * i, 2)]
            m_mine = two[:, :, pl.ds(pl.multiple_of(here * wide, wide), wide)].reshape(2 * half, wide)
            m_other = two[:, :, pl.ds(pl.multiple_of((1 - here) * wide, wide), wide)].reshape(2 * half, wide)
            for b in range(blocks):
                proj = lax.dot_general(mine[b][...], m_mine, NT, preferred_element_type=f32)
                proj += lax.dot_general(other[b][...], m_other, NT, preferred_element_type=f32)
                for at, part in enumerate(split2(proj)):
                    for j in range(2):
                        rows = pl.ds((2 * at + j) * width, width)
                        for s in range(2):
                            held[n, b, rows, s * half : (s + 1) * half] = part[
                                s * width : (s + 1) * width, j * half : (j + 1) * half
                            ]
        for n in range(sets):
            pair = info[1 + n] + i
            for b in range(blocks):
                high, low = held[n, b, : 2 * width, :], held[n, b, 2 * width :, :]
                add = jnp.dot(table[pair, :, : 2 * width], high, preferred_element_type=f32)
                add += jnp.dot(table[pair, :, 2 * width :], high, preferred_element_type=f32)
                add += jnp.dot(table[pair, :, : 2 * width], low, preferred_element_type=f32)
                after[b][...] += add


def add_blocks(info, mine, other, mats, table, totals):
    blocks, sets, fresh = len(mine), len(mats), totals is None
    half = mats[0].shape[1]
    height, tw = table.shape[1:]
    total = jax.ShapeDtypeStruct((height, 2 * half), f32)
    units = blocks * sets * mats[0].shape[0] // 2
    return pl.pallas_call(
        functools.partial(blocks_kernel, blocks, sets, fresh),
        in_specs=[SM] + [VM] * (2 * blocks + sets + 1 + (0 if fresh else blocks)),
        out_specs=[VM] * blocks,
        out_shape=[total] * blocks,
        scratch_shapes=[pltpu.VMEM((sets, blocks, tw, 2 * half), bf16)],
        input_output_aliases={} if fresh else {1 + 2 * blocks + sets + 1 + b: b for b in range(blocks)},
        compiler_params=params(),
        cost_estimate=pl.CostEstimate(flops=int(units * 0.69e9), bytes_accessed=0, transcendentals=0),
        name="add_blocks",
    )(info, *mine, *other, *mats, table, *([] if fresh else totals))


def finish_kernel(count, ways, info, *refs):
    totals, (edge, decay) = refs[:count], refs[count : count + 2]
    outs = refs[count + 2 : 2 * count + 2]
    held, entering, sems = refs[2 * count + 2 :]
    copies = [pltpu.make_async_copy(totals[s], held.at[info[s]], sems.at[s]) for s in range(count)]
    for c in copies:
        c.start()
    width, poles = edge.shape
    half = held.shape[2] // 2
    eh, el = split2(edge[...])
    left = jnp.concatenate([eh, el, eh], axis=1)
    for c in copies:
        c.wait()
    carried = jnp.zeros((poles, half), f32)
    for c in reversed(range(count)):
        state = held[c, width:, :]
        inner = state[:, half:] + decay[...] * carried
        ch, cl = split2(jnp.concatenate([inner, carried], axis=1))
        entering[c] = jnp.concatenate([ch, ch, cl], axis=0)
        carried = state[:, :half] + decay[...] * inner
    for n in range(count):
        c = info[count + n]
        value = held[c, :width, :] + jnp.dot(left, entering[c], preferred_element_type=f32)
        outs[n][:width, :] = value[:, :half]
        outs[n][width:, :] = value[:, half:]


def finish(info, totals, edge, decay, ways):
    count = len(totals)
    height, tw = totals[0].shape
    width, poles = edge.shape
    return pl.pallas_call(
        functools.partial(finish_kernel, count, ways),
        in_specs=[SM] + [ANY] * count + [VM, VM],
        out_specs=[VM] * count,
        out_shape=[jax.ShapeDtypeStruct((2 * width, tw // 2), f32)] * count,
        scratch_shapes=[
            pltpu.VMEM((count, height, tw), f32),
            pltpu.VMEM((count, 3 * poles, tw), bf16),
            pltpu.SemaphoreType.DMA((count,)),
        ],
        compiler_params=params(),
        cost_estimate=pl.CostEstimate(flops=int(3e9), bytes_accessed=0, transcendentals=0),
        name="finish_blocks",
    )(info, *totals, edge, decay)


def combine_kernel(*refs):
    value = refs[0][...]
    for r in refs[1:-1]:
        value = value + r[...]
    refs[-1][...] = value.astype(bf16)


def combine(parts):
    return pl.pallas_call(
        combine_kernel,
        in_specs=[VM] * len(parts),
        out_specs=VM,
        out_shape=jax.ShapeDtypeStruct(parts[0].shape, bf16),
        compiler_params=params(),
        name="combine_ways",
    )(*parts)


def arrange_kernel(count, info, *refs):
    out = refs[count]
    lanes = refs[0].shape[1]
    for r in range(count):
        out[:, pl.ds(pl.multiple_of(info[r] * lanes, lanes), lanes)] = refs[r][...]


def arrange(info, parts):
    rows, lanes = parts[0].shape
    return pl.pallas_call(
        functools.partial(arrange_kernel, len(parts)),
        in_specs=[SM] + [VM] * len(parts),
        out_specs=VM,
        out_shape=jax.ShapeDtypeStruct((rows, lanes * len(parts)), bf16),
        compiler_params=params(),
        name="arrange_features",
    )(info, *parts)


def plain_tables(coeffs, rates, gains, width):
    lag = jnp.arange(width, dtype=f32)
    decay = jnp.exp(-rates[:, None] * lag[None, :])
    shift = lag[None, :] - lag[:, None]
    phi = jnp.dot(coeffs * gains[None, :], decay, precision=exact_prec)
    near = jnp.where(shift >= 0, phi[:, jnp.maximum(shift, 0).astype(jnp.int32)], 0.0)
    return jnp.concatenate([near, coeffs[:, :, None] * decay[None]], axis=1)


def plain_cut(mats, info, plan, half, cols):
    return [
        lax.dynamic_slice(mats, (lo, info[2 * i], info[2 * i + 1]), (n, half, cols)) for i, (lo, n) in enumerate(plan)
    ]


def plain_add(info, mine, other, mats, table, totals):
    results = []
    wide, width = mine[0].shape[1], table.shape[2]
    for b in range(len(mine)):
        rows = jnp.concatenate([mine[b], other[b]], axis=1)
        total = 0.0 if totals is None else totals[b]
        for n in range(len(mats)):
            use = lax.dynamic_slice_in_dim(table, 2 * info[1 + n], mats[n].shape[0], 0)
            swapped = jnp.where(info[0] == 0, mats[n], jnp.roll(mats[n], wide, axis=2))
            proj = jnp.einsum("tj,kij->kti", rows, swapped, preferred_element_type=f32)
            proj = jnp.concatenate([proj[:, :width], proj[:, width:]], axis=2)
            total = total + jnp.einsum("kst,kti->si", use, proj, precision=exact_prec)
        results.append(total)
    return results


def plain_finish(info, totals, edge, decay, ways):
    count = len(totals)
    width, half = edge.shape[0], totals[0].shape[1] // 2
    held = jnp.zeros((count,) + totals[0].shape, f32)
    for s in range(count):
        held = lax.dynamic_update_slice(held, totals[s][None], (info[s], 0, 0))
    carried, values = jnp.zeros((edge.shape[1], half), f32), [None] * count
    for c in reversed(range(count)):
        state = held[c, width:]
        inner = state[:, half:] + decay * carried
        far = jnp.dot(edge, jnp.concatenate([inner, carried], axis=1), precision=exact_prec)
        value = held[c, :width] + far
        values[c] = jnp.concatenate([value[:, :half], value[:, half:]], axis=0)
        carried = state[:, :half] + decay * inner
    values = jnp.stack(values)
    return [values[info[count + n]] for n in range(count)]


def plain_combine(parts):
    return sum(parts[1:], parts[0]).astype(bf16)


def plain_arrange(info, parts):
    rows, lanes = parts[0].shape
    out = jnp.zeros((rows, lanes * len(parts)), bf16)
    for r, part in enumerate(parts):
        out = lax.dynamic_update_slice(out, part, (0, info[r] * lanes))
    return out


def per_device(out_grad, filter_mats, coeffs, pole_rates):
    count, groups = lax.axis_size("ctx"), lax.axis_size("grp")
    ways, per_grp = groups // 2, count // groups
    per = count // ways
    own_filters, features, _ = filter_mats.shape
    length, wide = out_grad.shape
    half, width = features // 2, length // 2
    kernels = half % 128 == 0 and wide % 128 == 0 and width % 256 == 0 and pole_rates.shape[0] % 16 == 0
    make, slices, add, end, both, put = (
        (tables, cut, add_blocks, finish, combine, arrange)
        if kernels
        else (plain_tables, plain_cut, plain_add, plain_finish, plain_combine, plain_arrange)
    )

    order = [*range(0, count, 2), *reversed(range(1, count, 2))]
    right = [(order[i], order[(i + 1) % count]) for i in range(count)]
    left = [(b, a) for a, b in right]
    offsets = [0]
    for step in range(1, count // 2):
        offsets += [-step, step]
    offsets.append(count // 2)
    far_ways = [(w, h) for w in range(1, ways) for h in range(2)]
    plan = [(lo, 2) for lo in range(0, own_filters, 2) for _ in far_ways] + [(0, own_filters)] * 2
    to = far_ways * (own_filters // 2) + [(0, 1), (0, 0)]

    def numbers(ctx, grp):
        way, here, at = grp // 2, grp % 2, order.index(ctx)
        cuts, firsts, near_firsts = [], [], []
        for w, h in to:
            cuts += [(here ^ h) * half, (way + w) % ways * 2 * wide]
        pair = lambda w, h, lo: (((way - w) % ways) * 2 + (here ^ h)) * (own_filters // 2) + lo // 2
        firsts = [[here] + [pair(w, h, lo) for w, h in far_ways] for lo in range(0, own_filters, 2)]
        near_firsts = [here, pair(0, 1, 0), pair(0, 0, 0)]
        turn = ctx % per_grp * 2 + here
        slots = [order[(at + o) % count] for o in offsets]
        use = [ways * ((r + turn) % per) + (way + w + ctx) % ways for w in range(ways) for r in range(per)]
        lanes = [(ctx // ways - r) % per for r in range(per)]
        return [cuts, near_firsts, *firsts, slots + use, lanes]

    rows = [numbers(c, g) for c in range(count) for g in range(groups)]
    ends = np.cumsum([len(part) for part in rows[0]])
    known = jnp.asarray(np.array([sum(r, []) for r in rows], np.int32))
    me = lax.axis_index("ctx") * groups + lax.axis_index("grp")
    row = lax.dynamic_slice(known, (me, 0), (1, known.shape[1]))[0]
    cuts, near_info, *rest = [row[e - len(part) : e] for e, part in zip(ends, rows[0])]
    far_info, finish_info, lanes_info = rest[:-2], rest[-2], rest[-1]

    def over_grp(x, by_way, by_core):
        rank = lambda w, h: (w % ways) * 2 + h
        pairs = [(rank(w, h), rank(w + by_way, h ^ by_core)) for w in range(ways) for h in range(2)]
        return lax.ppermute(x, "grp", pairs)

    swap = lambda x: over_grp(x, 0, 1)

    mine, other = [out_grad], [swap(out_grad)]
    going_right, going_left = out_grad, out_grad
    for step in range(1, count // 2):
        going_right = lax.ppermute(going_right, "ctx", right)
        going_left = lax.ppermute(going_left, "ctx", left)
        mine += [going_right, going_left]
        other += [swap(going_right), swap(going_left)]
    last = jnp.concatenate(
        [lax.ppermute(going_right[:width], "ctx", right), lax.ppermute(going_left[width:], "ctx", left)]
    )
    mine.append(last)
    other.append(swap(last))

    pieces = slices(filter_mats, cuts, plan, half, 2 * wide)
    far = [over_grp(p, w, h) for p, (w, h) in zip(pieces, to[:-2])]
    near = [swap(pieces[-2]), pieces[-1]]

    gains = jnp.sqrt(-jnp.expm1(-2.0 * pole_rates))
    table = make(coeffs, pole_rates, gains, width)
    totals = [None] * count

    def run(slots, info, mats):
        have = None if totals[slots[0]] is None else [totals[s] for s in slots]
        got = add(info, [mine[s] for s in slots], [other[s] for s in slots], mats, table, have)
        for s, t in zip(slots, got):
            totals[s] = t

    twos = [[s, s + 1] for s in range(1, count - 1, 2)]
    for slots in [[0], *twos, [count - 1]]:
        run(slots, near_info, near)
    for i, info in enumerate(far_info):
        for slots in [*twos, [0, count - 1]]:
            run(slots, info, far[i * len(far_ways) : (i + 1) * len(far_ways)])

    step_back = jnp.arange(width, dtype=f32) - width
    edge = gains[None, :] * jnp.exp(step_back[:, None] * pole_rates[None, :])
    decay = jnp.exp(-width * pole_rates)[:, None]
    partial = end(finish_info, totals, edge, decay, ways)
    arrived = [[over_grp(partial[w * per + r], w, 0) for w in range(1, ways)] for r in range(per)]
    received = []
    for r in range(per):
        result = both([partial[r], *arrived[r]])
        pairs = []
        for c in range(count):
            for g in range(groups):
                m = (r + c % per_grp * 2 + g % 2) % per
                goal = ways * m + (g // 2 + c) % ways
                pairs.append((c * groups + g, goal * groups + c // per_grp))
        received.append(lax.ppermute(result, ("ctx", "grp"), pairs))
    return put(lanes_info, received)


def solution(mesh):
    placed = (P("ctx", "grp"), P("grp", "ctx", None), P(), P())
    return jax.shard_map(
        per_device, mesh=mesh, in_specs=placed, out_specs=P("ctx", "grp"), check_vma=False
    )
```

```python
import functools

import jax
import jax.numpy as jnp
import numpy as np
from jax import lax
from jax.experimental import pallas as pl
from jax.experimental.pallas import tpu as pltpu
from jax.sharding import PartitionSpec as P

exact_prec = lax.Precision.HIGHEST
f32, bf16 = jnp.float32, jnp.bfloat16
NT = (((1,), (1,)), ((), ()))
VM = pl.BlockSpec(memory_space=pltpu.VMEM)
ANY = pl.BlockSpec(memory_space=pl.ANY)
SM = pl.BlockSpec(memory_space=pltpu.SMEM)


def params(mib=16):
    return pltpu.CompilerParams(vmem_limit_bytes=mib * 2**20)


def split2(x):
    high = x.astype(bf16)
    return high, (x - high.astype(f32)).astype(bf16)


def tables_kernel(poles_ref, out):
    poles, width = poles_ref.shape[0], out.shape[2] // 4
    rate, gain = poles_ref[:, 0:1], poles_ref[:, 1:2]
    lag = lax.broadcasted_iota(jnp.int32, (poles, width), 1).astype(f32)
    decay = jnp.exp(-rate * lag)
    gained = gain * decay
    columns = lax.broadcasted_iota(jnp.int32, (poles, poles_ref.shape[1]), 1)

    @pl.loop(0, out.shape[0])
    def _(pair):
        for j in range(2):
            chosen = jnp.where(columns == 2 + 2 * pair + j, poles_ref[...], 0.0)
            coef = jnp.sum(chosen, axis=1, keepdims=True)
            phi = jnp.sum(coef * gained, axis=0, keepdims=True)
            line = jnp.concatenate([phi, jnp.zeros((1, width), f32)], axis=1)
            rolled = pltpu.roll(jnp.broadcast_to(line, (width, 2 * width)), 0, 1, stride=1, stride_axis=0)
            near, weight = split2(rolled[:, :width]), split2(coef * decay)
            for at in range(2):
                lanes = slice((2 * at + j) * width, (2 * at + j + 1) * width)
                out[pair, :width, lanes] = near[at]
                out[pair, width:, lanes] = weight[at]


def tables(coeffs, rates, gains, width):
    filters, poles = coeffs.shape
    joined = jnp.concatenate([rates[:, None], gains[:, None], coeffs.T], axis=1)
    return pl.pallas_call(
        tables_kernel,
        in_specs=[VM],
        out_specs=VM,
        out_shape=jax.ShapeDtypeStruct((filters // 2, width + poles, 4 * width), bf16),
        compiler_params=params(),
        cost_estimate=pl.CostEstimate(flops=int(4e9), bytes_accessed=0, transcendentals=0),
        name="pole_tables",
    )(joined)


def cut_kernel(plan, info, mats, *refs):
    outs, sems = refs[:-1], refs[-1]
    copies = []
    for i, (lo, n) in enumerate(plan):
        half, cols = outs[i].shape[1:]
        src = mats.at[
            pl.ds(lo, n),
            pl.ds(pl.multiple_of(info[2 * i], half), half),
            pl.ds(pl.multiple_of(info[2 * i + 1], cols), cols),
        ]
        copies.append(pltpu.make_async_copy(src, outs[i], sems.at[i]))
    for c in copies:
        c.start()
    for c in copies:
        c.wait()


def cut(mats, info, plan, half, cols):
    return pl.pallas_call(
        functools.partial(cut_kernel, plan),
        in_specs=[SM, ANY],
        out_specs=[VM] * len(plan),
        out_shape=[jax.ShapeDtypeStruct((n, half, cols), bf16) for _, n in plan],
        scratch_shapes=[pltpu.SemaphoreType.DMA((len(plan),))],
        compiler_params=params(60),
        name="cut_filters",
    )(info, mats)


def blocks_kernel(blocks, sets, fresh, info, *refs):
    mine, other = refs[:blocks], refs[blocks : 2 * blocks]
    mats = refs[2 * blocks : 2 * blocks + sets]
    table = refs[2 * blocks + sets]
    rest = refs[2 * blocks + sets + 1 :]
    before, after, held = rest[:-blocks - 1], rest[-blocks - 1 : -1], rest[-1]
    wide = mine[0].shape[1]
    here = info[0]
    width = table.shape[2] // 4
    half = mats[0].shape[1]
    subs = mine[0].shape[0] // width
    pairs = mats[0].shape[0] // 2
    units = [(i, n, b) for i in range(pairs) for n in range(sets) for b in range(blocks)]
    for u, (i, n, b) in enumerate(units):
        two = mats[n].at[pl.ds(2 * i, 2)]
        m_mine = two[:, :, pl.ds(pl.multiple_of(here * wide, wide), wide)].reshape(2 * half, wide)
        m_other = two[:, :, pl.ds(pl.multiple_of((1 - here) * wide, wide), wide)].reshape(2 * half, wide)
        proj = lax.dot_general(mine[b][...], m_mine, NT, preferred_element_type=f32)
        proj += lax.dot_general(other[b][...], m_other, NT, preferred_element_type=f32)
        for at, part in enumerate(split2(proj)):
            for j in range(2):
                rows = pl.ds((2 * at + j) * width, width)
                for s in range(subs):
                    held[u, rows, s * half : (s + 1) * half] = part[
                        s * width : (s + 1) * width, j * half : (j + 1) * half
                    ]
    for u, (i, n, b) in enumerate(units):
        pair = info[1 + n] + i
        high, low = held[u, : 2 * width, :], held[u, 2 * width :, :]
        add = jnp.dot(table[pair, :, : 2 * width], high, preferred_element_type=f32)
        add += jnp.dot(table[pair, :, 2 * width :], high, preferred_element_type=f32)
        add += jnp.dot(table[pair, :, : 2 * width], low, preferred_element_type=f32)
        if fresh and i == n == 0:
            after[b][...] = add
        elif i == n == 0:
            after[b][...] = before[b][...] + add
        else:
            after[b][...] += add


def add_blocks(info, mine, other, mats, table, totals):
    blocks, sets, fresh = len(mine), len(mats), totals is None
    half = mats[0].shape[1]
    height, tw = table.shape[1:]
    lanes = mine[0].shape[0] // (tw // 4) * half
    total = jax.ShapeDtypeStruct((height, lanes), f32)
    units = blocks * sets * mats[0].shape[0] // 2
    return pl.pallas_call(
        functools.partial(blocks_kernel, blocks, sets, fresh),
        in_specs=[SM] + [VM] * (2 * blocks + sets + 1 + (0 if fresh else blocks)),
        out_specs=[VM] * blocks,
        out_shape=[total] * blocks,
        scratch_shapes=[pltpu.VMEM((units, tw, lanes), bf16)],
        input_output_aliases={} if fresh else {1 + 2 * blocks + sets + 1 + b: b for b in range(blocks)},
        compiler_params=params(),
        cost_estimate=pl.CostEstimate(flops=int(units * 0.6e9), bytes_accessed=0, transcendentals=0),
        name="add_blocks",
    )(info, *mine, *other, *mats, table, *([] if fresh else totals))


def finish_kernel(count, info, *refs):
    totals, (edge, decay) = refs[:count], refs[count : count + 2]
    outs = refs[count + 2 : 2 * count + 2]
    held, entering, sems = refs[2 * count + 2 :]
    copies = [pltpu.make_async_copy(totals[s], held.at[info[s]], sems.at[s]) for s in range(count)]
    for c in copies:
        c.start()
    width, poles = edge.shape
    subs = outs[0].shape[0] // width
    half = held.shape[2] // subs
    eh, el = split2(edge[...])
    left = jnp.concatenate([eh, el, eh], axis=1)
    for c in copies:
        c.wait()
    carried = jnp.zeros((poles, half), f32)
    for c in reversed(range(count)):
        state, enters = held[c, width:, :], []
        for s in reversed(range(subs)):
            enters.append(carried)
            carried = state[:, s * half : (s + 1) * half] + decay[...] * carried
        ch, cl = split2(jnp.concatenate(enters[::-1], axis=1))
        entering[c] = jnp.concatenate([ch, ch, cl], axis=0)
    for n in range(count):
        c = info[count + n]
        value = held[c, :width, :] + jnp.dot(left, entering[c], preferred_element_type=f32)
        for s in range(subs):
            outs[n][s * width : (s + 1) * width, :] = value[:, s * half : (s + 1) * half]


def finish(info, totals, edge, decay, length):
    count = len(totals)
    height, tw = totals[0].shape
    width, poles = edge.shape
    half = tw * width // length
    return pl.pallas_call(
        functools.partial(finish_kernel, count),
        in_specs=[SM] + [ANY] * count + [VM, VM],
        out_specs=[VM] * count,
        out_shape=[jax.ShapeDtypeStruct((length, half), f32)] * count,
        scratch_shapes=[
            pltpu.VMEM((count, height, tw), f32),
            pltpu.VMEM((count, 3 * poles, tw), bf16),
            pltpu.SemaphoreType.DMA((count,)),
        ],
        compiler_params=params(),
        cost_estimate=pl.CostEstimate(flops=int(3e9), bytes_accessed=0, transcendentals=0),
        name="finish_blocks",
    )(info, *totals, edge, decay)


def combine_kernel(*refs):
    value = refs[0][...]
    for r in refs[1:-1]:
        value = value + r[...]
    refs[-1][...] = value.astype(bf16)


def combine(parts):
    return pl.pallas_call(
        combine_kernel,
        in_specs=[VM] * len(parts),
        out_specs=VM,
        out_shape=jax.ShapeDtypeStruct(parts[0].shape, bf16),
        compiler_params=params(),
        name="combine_ways",
    )(*parts)


def arrange_kernel(count, info, *refs):
    out = refs[count]
    lanes = refs[0].shape[1]
    for r in range(count):
        out[:, pl.ds(pl.multiple_of(info[r] * lanes, lanes), lanes)] = refs[r][...]


def arrange(info, parts):
    rows, lanes = parts[0].shape
    return pl.pallas_call(
        functools.partial(arrange_kernel, len(parts)),
        in_specs=[SM] + [VM] * len(parts),
        out_specs=VM,
        out_shape=jax.ShapeDtypeStruct((rows, lanes * len(parts)), bf16),
        compiler_params=params(),
        name="arrange_features",
    )(info, *parts)


def plain_tables(coeffs, rates, gains, width):
    lag = jnp.arange(width, dtype=f32)
    decay = jnp.exp(-rates[:, None] * lag[None, :])
    shift = lag[None, :] - lag[:, None]
    phi = jnp.dot(coeffs * gains[None, :], decay, precision=exact_prec)
    near = jnp.where(shift >= 0, phi[:, jnp.maximum(shift, 0).astype(jnp.int32)], 0.0)
    return jnp.concatenate([near, coeffs[:, :, None] * decay[None]], axis=1)


def plain_cut(mats, info, plan, half, cols):
    return [
        lax.dynamic_slice(mats, (lo, info[2 * i], info[2 * i + 1]), (n, half, cols)) for i, (lo, n) in enumerate(plan)
    ]


def plain_add(info, mine, other, mats, table, totals):
    results = []
    wide, width = mine[0].shape[1], table.shape[2]
    for b in range(len(mine)):
        rows = jnp.concatenate([mine[b], other[b]], axis=1)
        total = 0.0 if totals is None else totals[b]
        for n in range(len(mats)):
            use = lax.dynamic_slice_in_dim(table, 2 * info[1 + n], mats[n].shape[0], 0)
            swapped = jnp.where(info[0] == 0, mats[n], jnp.roll(mats[n], wide, axis=2))
            proj = jnp.einsum("tj,kij->kti", rows, swapped, preferred_element_type=f32)
            proj = jnp.concatenate(jnp.split(proj, rows.shape[0] // width, axis=1), axis=2)
            total = total + jnp.einsum("kst,kti->si", use, proj, precision=exact_prec)
        results.append(total)
    return results


def plain_finish(info, totals, edge, decay, length):
    count, width = len(totals), edge.shape[0]
    subs = length // width
    held = jnp.zeros((count,) + totals[0].shape, f32)
    for s in range(count):
        held = lax.dynamic_update_slice(held, totals[s][None], (info[s], 0, 0))
    carried, values = jnp.zeros((edge.shape[1], totals[0].shape[1] // subs), f32), [None] * count
    for c in reversed(range(count)):
        enters = []
        for state in reversed(jnp.split(held[c, width:], subs, axis=1)):
            enters.append(carried)
            carried = state + decay * carried
        far = jnp.dot(edge, jnp.concatenate(enters[::-1], axis=1), precision=exact_prec)
        values[c] = jnp.concatenate(jnp.split(held[c, :width] + far, subs, axis=1), axis=0)
    values = jnp.stack(values)
    return [values[info[count + n]] for n in range(count)]


def plain_combine(parts):
    return sum(parts[1:], parts[0]).astype(bf16)


def plain_arrange(info, parts):
    rows, lanes = parts[0].shape
    out = jnp.zeros((rows, lanes * len(parts)), bf16)
    for r, part in enumerate(parts):
        out = lax.dynamic_update_slice(out, part, (0, info[r] * lanes))
    return out


def per_device(out_grad, filter_mats, coeffs, pole_rates):
    count, groups = lax.axis_size("ctx"), lax.axis_size("grp")
    ways, per_grp = groups // 2, count // groups
    per = count // ways
    own_filters, features, _ = filter_mats.shape
    length, wide = out_grad.shape
    half, width = features // 2, length // 4
    kernels = half % 128 == 0 and wide % 128 == 0 and width % 128 == 0 and pole_rates.shape[0] % 16 == 0
    make, slices, add, end, both, put = (
        (tables, cut, add_blocks, finish, combine, arrange)
        if kernels
        else (plain_tables, plain_cut, plain_add, plain_finish, plain_combine, plain_arrange)
    )

    order = [*range(0, count, 2), *reversed(range(1, count, 2))]
    right = [(order[i], order[(i + 1) % count]) for i in range(count)]
    left = [(b, a) for a, b in right]
    offsets = [0]
    for step in range(1, count // 2):
        offsets += [-step, step]
    offsets.append(count // 2)
    far_ways = [(w, h) for w in range(1, ways) for h in range(2)]
    plan = [(0, own_filters)] * (len(far_ways) + 2)
    to = far_ways + [(0, 1), (0, 0)]

    def numbers(ctx, grp):
        way, here, at = grp // 2, grp % 2, order.index(ctx)
        cuts = []
        for w, h in to:
            cuts += [(here ^ h) * half, (way + w) % ways * 2 * wide]
        pair = lambda w, h: (((way - w) % ways) * 2 + (here ^ h)) * (own_filters // 2)
        firsts = [[here, pair(w, h)] for w, h in far_ways]
        near_firsts = [here, pair(0, 1), pair(0, 0)]
        turn = ctx % per_grp * 2 + here
        slots = [order[(at + o) % count] for o in offsets]
        use = [ways * ((r + turn) % per) + (way + w + ctx) % ways for w in range(ways) for r in range(per)]
        lanes = [(ctx // ways - r) % per for r in range(per)]
        every = near_firsts + [f[1] for f in firsts]
        return [cuts, near_firsts, *firsts, every, slots + use, lanes]

    rows = [numbers(c, g) for c in range(count) for g in range(groups)]
    ends = np.cumsum([len(part) for part in rows[0]])
    known = jnp.asarray(np.array([sum(r, []) for r in rows], np.int32))
    me = lax.axis_index("ctx") * groups + lax.axis_index("grp")
    row = lax.dynamic_slice(known, (me, 0), (1, known.shape[1]))[0]
    cuts, near_info, *rest = [row[e - len(part) : e] for e, part in zip(ends, rows[0])]
    far_info, (every_info, finish_info, lanes_info) = rest[:-3], rest[-3:]

    def over_grp(x, by_way, by_core):
        rank = lambda w, h: (w % ways) * 2 + h
        pairs = [(rank(w, h), rank(w + by_way, h ^ by_core)) for w in range(ways) for h in range(2)]
        return lax.ppermute(x, "grp", pairs)

    swap = lambda x: over_grp(x, 0, 1)

    mine, other = [out_grad], [swap(out_grad)]
    going_right, going_left = out_grad, out_grad
    for step in range(1, count // 2):
        going_right = lax.ppermute(going_right, "ctx", right)
        going_left = lax.ppermute(going_left, "ctx", left)
        mine += [going_right, going_left]
        other += [swap(going_right), swap(going_left)]
    last = jnp.concatenate(
        [lax.ppermute(going_right[: length // 2], "ctx", right), lax.ppermute(going_left[length // 2 :], "ctx", left)]
    )
    mine.append(last)
    other.append(swap(last))

    pieces = slices(filter_mats, cuts, plan, half, 2 * wide)
    far = []
    for p, (w, h) in zip(pieces, to[:-2]):
        if far:
            p, far[-1] = lax.optimization_barrier((p, far[-1]))
        far.append(over_grp(p, w, h))
    near = [swap(pieces[-2]), pieces[-1]]

    gains = jnp.sqrt(-jnp.expm1(-2.0 * pole_rates))
    table = make(coeffs, pole_rates, gains, width)
    totals = [None] * count

    def run(slots, info, mats):
        have = None if totals[slots[0]] is None else [totals[s] for s in slots]
        got = add(info, [mine[s] for s in slots], [other[s] for s in slots], mats, table, have)
        for s, t in zip(slots, got):
            totals[s] = t

    twos = [[s, s + 1] for s in range(1, count - 1, 2)]
    for slots in [[0], *twos]:
        run(slots, near_info, near)
    early = [0, *range(1, count - 1)]
    for i in range(len(far)):
        for at in range(0, count - 1, 4):
            run(early[at : at + 4], far_info[i], [far[i]])
    run([count - 1], every_info, [*near, *far])

    step_back = jnp.arange(width, dtype=f32) - width
    edge = gains[None, :] * jnp.exp(step_back[:, None] * pole_rates[None, :])
    decay = jnp.exp(-width * pole_rates)[:, None]
    partial = end(finish_info, totals, edge, decay, length)
    arrived = [[over_grp(partial[w * per + r], w, 0) for w in range(1, ways)] for r in range(per)]
    received = []
    for r in range(per):
        result = both([partial[r], *arrived[r]])
        pairs = []
        for c in range(count):
            for g in range(groups):
                m = (r + c % per_grp * 2 + g % 2) % per
                goal = ways * m + (g // 2 + c) % ways
                pairs.append((c * groups + g, goal * groups + c // per_grp))
        received.append(lax.ppermute(result, ("ctx", "grp"), pairs))
    return put(lanes_info, received)


def solution(mesh):
    placed = (P("ctx", "grp"), P("grp", "ctx", None), P(), P())
    return jax.shard_map(
        per_device, mesh=mesh, in_specs=placed, out_specs=P("ctx", "grp"), check_vma=False
    )
```

```python
import functools
import random

import jax
import jax.numpy as jnp
import numpy as np
from jax import lax
from jax.experimental import pallas as pl
from jax.experimental.pallas import tpu as pltpu
from jax.sharding import PartitionSpec as P

exact_prec = lax.Precision.HIGHEST
f32, bf16 = jnp.float32, jnp.bfloat16
NT = (((1,), (1,)), ((), ()))
VM = pl.BlockSpec(memory_space=pltpu.VMEM)
ANY = pl.BlockSpec(memory_space=pl.ANY)
SM = pl.BlockSpec(memory_space=pltpu.SMEM)


def params(mib=16):
    return pltpu.CompilerParams(vmem_limit_bytes=mib * 2**20)


def split2(x):
    high = x.astype(bf16)
    return high, (x - high.astype(f32)).astype(bf16)


def tables_kernel(poles_ref, out):
    poles, width = poles_ref.shape[0], out.shape[2] // 4
    rate, gain = poles_ref[:, 0:1], poles_ref[:, 1:2]
    lag = lax.broadcasted_iota(jnp.int32, (poles, width), 1).astype(f32)
    decay = jnp.exp(-rate * lag)
    gained = gain * decay
    columns = lax.broadcasted_iota(jnp.int32, (poles, poles_ref.shape[1]), 1)

    @pl.loop(0, out.shape[0])
    def _(pair):
        for j in range(2):
            chosen = jnp.where(columns == 2 + 2 * pair + j, poles_ref[...], 0.0)
            coef = jnp.sum(chosen, axis=1, keepdims=True)
            phi = jnp.sum(coef * gained, axis=0, keepdims=True)
            line = jnp.concatenate([phi, jnp.zeros((1, width), f32)], axis=1)
            rolled = pltpu.roll(jnp.broadcast_to(line, (width, 2 * width)), 0, 1, stride=1, stride_axis=0)
            near, weight = split2(rolled[:, :width]), split2(coef * decay)
            for at in range(2):
                lanes = slice((2 * at + j) * width, (2 * at + j + 1) * width)
                out[pair, :width, lanes] = near[at]
                out[pair, width:, lanes] = weight[at]


def tables(coeffs, rates, gains, width):
    filters, poles = coeffs.shape
    joined = jnp.concatenate([rates[:, None], gains[:, None], coeffs.T], axis=1)
    return pl.pallas_call(
        tables_kernel,
        in_specs=[VM],
        out_specs=VM,
        out_shape=jax.ShapeDtypeStruct((filters // 2, width + poles, 4 * width), bf16),
        compiler_params=params(),
        cost_estimate=pl.CostEstimate(flops=int(4e9), bytes_accessed=0, transcendentals=0),
        name="pole_tables",
    )(joined)


def cut_kernel(to, mats, *refs):
    outs, sems = refs[:-1], refs[-1]
    way, here = lax.axis_index("grp") // 2, lax.axis_index("grp") % 2
    copies = []
    for i, (by_way, by_core) in enumerate(to):
        _, half, cols = outs[i].shape
        row = (1 - here if by_core else here) * half
        col = (1 - way if by_way else way) * cols
        src = mats.at[:, pl.ds(pl.multiple_of(row, half), half), pl.ds(pl.multiple_of(col, cols), cols)]
        copies.append(pltpu.make_async_copy(src, outs[i], sems.at[i]))
    for c in copies:
        c.start()
    for c in copies:
        c.wait()


def cut(mats, to, half, cols):
    return pl.pallas_call(
        functools.partial(cut_kernel, to),
        in_specs=[ANY],
        out_specs=[VM] * len(to),
        out_shape=[jax.ShapeDtypeStruct((mats.shape[0], half, cols), bf16)] * len(to),
        scratch_shapes=[pltpu.SemaphoreType.DMA((len(to),))],
        compiler_params=params(60),
        name="cut_filters",
    )(mats)


def products(work, info_at, info, mine, other, mats, table, before, after, held):
    wide = mine[0].shape[1]
    here = info[info_at[0]]
    width = table.shape[2] // 4
    half = mats[0].shape[1]
    subs = mine[0].shape[0] // width
    units = [(i, n, b) for i in range(mats[0].shape[0] // 2) for n, b in work]
    for u, (i, n, b) in enumerate(units):
        two = mats[n].at[pl.ds(2 * i, 2)]
        m_mine = two[:, :, pl.ds(pl.multiple_of(here * wide, wide), wide)].reshape(2 * half, wide)
        m_other = two[:, :, pl.ds(pl.multiple_of((1 - here) * wide, wide), wide)].reshape(2 * half, wide)
        proj = lax.dot_general(mine[b][...], m_mine, NT, preferred_element_type=f32)
        proj += lax.dot_general(other[b][...], m_other, NT, preferred_element_type=f32)
        for at, part in enumerate(split2(proj)):
            for j in range(2):
                rows = pl.ds((2 * at + j) * width, width)
                for s in range(subs):
                    held[u, rows, s * half : (s + 1) * half] = part[
                        s * width : (s + 1) * width, j * half : (j + 1) * half
                    ]
    begun = set()
    for u, (i, n, b) in enumerate(units):
        pair = info[info_at[1 + n]] + i
        high, low = held[u, : 2 * width, :], held[u, 2 * width :, :]
        add = jnp.dot(table[pair, :, : 2 * width], high, preferred_element_type=f32)
        add += jnp.dot(table[pair, :, 2 * width :], high, preferred_element_type=f32)
        add += jnp.dot(table[pair, :, : 2 * width], low, preferred_element_type=f32)
        if b in begun:
            after[b][...] += add
        else:
            after[b][...] = add if before[b] is None else before[b][...] + add
            begun.add(b)


def blocks_kernel(blocks, sets, work, info_at, fresh, closing, info, *refs):
    refs = list(refs)
    take = lambda n: [refs.pop(0) for _ in range(n)]
    mine, other, mats, (table,) = take(blocks), take(blocks), take(sets), take(1)
    before = [None if new else refs.pop(0) for new in fresh]
    if not closing:
        after, (held,) = take(blocks), take(1)
        products(work, info_at, info, mine, other, mats, table, before, after, held)
        return
    edge, decay, kept, sent, *states = take(4 + blocks)
    held, after = refs
    after = [after.at[b] for b in range(blocks)]
    products(work, info_at, info, mine, other, mats, table, before, after, held)
    width, poles = edge.shape
    half = mats[0].shape[1]
    subs = mine[0].shape[0] // width
    eh, el = split2(edge[...])
    left = jnp.concatenate([eh, el, eh], axis=1)
    values = []
    for b in range(blocks):
        state, enters, carried = after[b][width:, :], [], jnp.zeros((poles, half), f32)
        for s in reversed(range(subs)):
            enters.append(carried)
            carried = state[:, s * half : (s + 1) * half] + decay[...] * carried
        states[b][...] = carried
        ch, cl = split2(jnp.concatenate(enters[::-1], axis=1))
        far = jnp.dot(left, jnp.concatenate([ch, ch, cl], axis=0), preferred_element_type=f32)
        values.append(after[b][:width, :] + far)
    first = info[closing] == 0
    for ref, one, two in ((kept, *values), (sent, *reversed(values))):
        value = jnp.where(first, one, two)
        for s in range(subs):
            ref[s * width : (s + 1) * width, :] = value[:, s * half : (s + 1) * half]


def add_blocks(info, info_at, mine, other, mats, table, totals, work, ends=None, closing=0):
    blocks, sets = len(mine), len(mats)
    fresh = [t is None for t in totals]
    old = [t for t in totals if t is not None]
    half, length = mats[0].shape[1], mine[0].shape[0]
    height, tw = table.shape[1:]
    lanes = length // (tw // 4) * half
    units = len(work) * mats[0].shape[0] // 2
    first = 1 + 2 * blocks + sets + 1
    scratch = [pltpu.VMEM((units, tw, lanes), bf16)]
    if ends is None:
        ends, aliases = (), {first + i: b for i, b in enumerate(b for b in range(blocks) if not fresh[b])}
        shapes = [jax.ShapeDtypeStruct((height, lanes), f32)] * blocks
    else:
        aliases = {}
        shapes = [jax.ShapeDtypeStruct((length, half), f32)] * 2
        shapes += [jax.ShapeDtypeStruct((height - tw // 4, half), f32)] * blocks
        scratch.append(pltpu.VMEM((blocks, height, lanes), f32))
    return pl.pallas_call(
        functools.partial(blocks_kernel, blocks, sets, work, info_at, fresh, closing),
        in_specs=[SM] + [VM] * (2 * blocks + sets + 1 + len(old) + len(ends)),
        out_specs=[VM] * len(shapes),
        out_shape=shapes,
        scratch_shapes=scratch,
        input_output_aliases=aliases,
        compiler_params=params(24 if closing else 16),
        cost_estimate=pl.CostEstimate(flops=int(units * 0.6e9), bytes_accessed=0, transcendentals=0),
        name="close_blocks" if closing else "add_blocks",
    )(info, *mine, *other, *mats, table, *old, *ends)


def carry_kernel(count, slots_at, use_at, info, *refs):
    states, decay, (kept, sent), (held, entering) = refs[:count], refs[count], refs[count + 1 : count + 3], refs[count + 3 :]
    for s in range(count):
        held[info[slots_at + s]] = states[s][...]
    carried = jnp.zeros_like(states[0])
    for c in reversed(range(count)):
        entering[c] = carried
        carried = held[c] + decay[...] * carried
    per = kept.shape[0]
    for r in range(per):
        kept[r] = entering[info[use_at + r]]
        sent[r] = entering[info[use_at + per + r]]


def carry(info, slots_at, use_at, states, decay):
    count, shape = len(states), states[0].shape
    return pl.pallas_call(
        functools.partial(carry_kernel, count, slots_at, use_at),
        in_specs=[SM] + [VM] * (count + 1),
        out_specs=[VM] * 2,
        out_shape=[jax.ShapeDtypeStruct((count // 2, *shape), f32)] * 2,
        scratch_shapes=[pltpu.VMEM((count, *shape), f32)] * 2,
        compiler_params=params(),
        name="carry_states",
    )(info, *states, decay)


def result_kernel(pairs, here_at, info, *refs):
    kept, arrived = refs[: len(pairs)], refs[len(pairs) : 2 * len(pairs)]
    carry_kept, carry_arrived, edge, *outs = refs[2 * len(pairs) :]
    eh, el = split2(edge[...])
    left = jnp.concatenate([eh, el, eh], axis=1)
    values = []
    for n, r in enumerate(pairs):
        ch, cl = split2(carry_kept[r] + carry_arrived[r])
        far = jnp.dot(left, jnp.concatenate([ch, ch, cl], axis=0), preferred_element_type=f32)
        values.append((kept[n][...] + arrived[n][...] + far).astype(bf16))
    first = info[here_at] == 0
    outs[0][...] = jnp.where(first, values[0], values[1])
    outs[1][...] = jnp.where(first, values[1], values[0])


def results(info, here_at, pairs, kept, arrived, carries, edge):
    return pl.pallas_call(
        functools.partial(result_kernel, pairs, here_at),
        in_specs=[SM] + [VM] * (2 * len(pairs) + 3),
        out_specs=[VM] * len(pairs),
        out_shape=[jax.ShapeDtypeStruct(kept[0].shape, bf16)] * len(pairs),
        compiler_params=params(),
        name="finish_blocks",
    )(info, *kept, *arrived, *carries, edge)


def arrange_kernel(count, lanes_at, info, *refs):
    out = refs[count]
    lanes = refs[0].shape[1]
    for r in range(count):
        out[:, pl.ds(pl.multiple_of(info[lanes_at + r] * lanes, lanes), lanes)] = refs[r][...]


def arrange(info, lanes_at, parts):
    rows, lanes = parts[0].shape
    return pl.pallas_call(
        functools.partial(arrange_kernel, len(parts), lanes_at),
        in_specs=[SM] + [VM] * len(parts),
        out_specs=VM,
        out_shape=jax.ShapeDtypeStruct((rows, lanes * len(parts)), bf16),
        compiler_params=params(),
        name="arrange_features",
    )(info, *parts)


def plain_tables(coeffs, rates, gains, width):
    lag = jnp.arange(width, dtype=f32)
    decay = jnp.exp(-rates[:, None] * lag[None, :])
    shift = lag[None, :] - lag[:, None]
    phi = jnp.dot(coeffs * gains[None, :], decay, precision=exact_prec)
    near = jnp.where(shift >= 0, phi[:, jnp.maximum(shift, 0).astype(jnp.int32)], 0.0)
    return jnp.concatenate([near, coeffs[:, :, None] * decay[None]], axis=1)


def plain_cut(mats, info, plan, half, cols):
    return [
        lax.dynamic_slice(mats, (lo, info[2 * i], info[2 * i + 1]), (n, half, cols)) for i, (lo, n) in enumerate(plan)
    ]


def plain_add(info, mine, other, mats, table, totals, work):
    results = []
    wide, width = mine[0].shape[1], table.shape[2]
    for b in range(len(mine)):
        rows = jnp.concatenate([mine[b], other[b]], axis=1)
        total = 0.0 if totals[b] is None else totals[b]
        for n in [n for n, at in work if at == b]:
            use = lax.dynamic_slice_in_dim(table, 2 * info[1 + n], mats[n].shape[0], 0)
            swapped = jnp.where(info[0] == 0, mats[n], jnp.roll(mats[n], wide, axis=2))
            proj = jnp.einsum("tj,kij->kti", rows, swapped, preferred_element_type=f32)
            proj = jnp.concatenate(jnp.split(proj, rows.shape[0] // width, axis=1), axis=2)
            total = total + jnp.einsum("kst,kti->si", use, proj, precision=exact_prec)
        results.append(total)
    return results


def plain_finish(info, totals, edge, decay, length):
    count, width = len(totals), edge.shape[0]
    subs = length // width
    held = jnp.zeros((count,) + totals[0].shape, f32)
    for s in range(count):
        held = lax.dynamic_update_slice(held, totals[s][None], (info[s], 0, 0))
    carried, values = jnp.zeros((edge.shape[1], totals[0].shape[1] // subs), f32), [None] * count
    for c in reversed(range(count)):
        enters = []
        for state in reversed(jnp.split(held[c, width:], subs, axis=1)):
            enters.append(carried)
            carried = state + decay * carried
        far = jnp.dot(edge, jnp.concatenate(enters[::-1], axis=1), precision=exact_prec)
        values[c] = jnp.concatenate(jnp.split(held[c, :width] + far, subs, axis=1), axis=0)
    values = jnp.stack(values)
    return [values[info[count + n]] for n in range(count)]


def plain_combine(parts):
    return sum(parts[1:], parts[0]).astype(bf16)


def plain_arrange(info, parts):
    rows, lanes = parts[0].shape
    out = jnp.zeros((rows, lanes * len(parts)), bf16)
    for r, part in enumerate(parts):
        out = lax.dynamic_update_slice(out, part, (0, info[r] * lanes))
    return out


def ring_of(count):
    order = [*range(0, count, 2), *reversed(range(1, count, 2))]
    offsets = [0]
    for step in range(1, count // 2):
        offsets += [-step, step]
    return order, [*offsets, count // 2]


def shift_of(x, ways, by_way, by_core):
    rank = lambda w, h: (w % ways) * 2 + h
    return lax.ppermute(x, "grp", [(rank(w, h), rank(w + by_way, h ^ by_core)) for w in range(ways) for h in range(2)])


def my_row(count, groups, numbers):
    rows = [numbers(c, g) for c in range(count) for g in range(groups)]
    ends = np.cumsum([len(part) for part in rows[0]])
    known = jnp.asarray(np.array([sum(r, []) for r in rows], np.int32))
    me = lax.axis_index("ctx") * groups + lax.axis_index("grp")
    row = lax.dynamic_slice(known, (me, 0), (1, known.shape[1]))[0]
    return row, [int(e) - len(part) for e, part in zip(ends, rows[0])], [int(e) for e in ends]


def plain_device(out_grad, filter_mats, coeffs, pole_rates):
    count, groups = lax.axis_size("ctx"), lax.axis_size("grp")
    ways, per_grp = groups // 2, count // groups
    per = count // ways
    own_filters, features, _ = filter_mats.shape
    length, wide = out_grad.shape
    half, width = features // 2, length // 4
    order, offsets = ring_of(count)
    right = [(order[i], order[(i + 1) % count]) for i in range(count)]
    left = [(b, a) for a, b in right]
    to = [(w, h) for w in range(1, ways) for h in range(2)] + [(0, 1), (0, 0)]
    plan = [(0, own_filters)] * len(to)

    def numbers(ctx, grp):
        way, here, at = grp // 2, grp % 2, order.index(ctx)
        cuts = []
        for w, h in to:
            cuts += [(here ^ h) * half, (way + w) % ways * 2 * wide]
        firsts = [(((way - w) % ways) * 2 + (here ^ h)) * (own_filters // 2) for w, h in to]
        turn = ctx % per_grp * 2 + here
        slots = [order[(at + o) % count] for o in offsets]
        use = [ways * ((r + turn) % per) + (way + w + ctx) % ways for w in range(ways) for r in range(per)]
        return [cuts, [here] + firsts, slots + use, [(ctx // ways - r) % per for r in range(per)]]

    row, begins, ends = my_row(count, groups, numbers)
    cuts, firsts, finish_info, lanes_info = [row[b:e] for b, e in zip(begins, ends)]
    swap = lambda x: shift_of(x, ways, 0, 1)
    mine, other = [out_grad], [swap(out_grad)]
    going_right, going_left = out_grad, out_grad
    for step in range(1, count // 2):
        going_right = lax.ppermute(going_right, "ctx", right)
        going_left = lax.ppermute(going_left, "ctx", left)
        mine += [going_right, going_left]
        other += [swap(going_right), swap(going_left)]
    mine.append(lax.ppermute(going_right, "ctx", right))
    other.append(swap(mine[-1]))
    pieces = plain_cut(filter_mats, cuts, plan, half, 2 * wide)
    mats = [shift_of(p, ways, w, h) for p, (w, h) in zip(pieces[:-1], to[:-1])] + pieces[-1:]
    gains = jnp.sqrt(-jnp.expm1(-2.0 * pole_rates))
    table = plain_tables(coeffs, pole_rates, gains, width)
    work = [(n, 0) for n in range(len(mats))]
    totals = [plain_add(firsts, [m], [o], mats, table, [None], work)[0] for m, o in zip(mine, other)]
    step_back = jnp.arange(width, dtype=f32) - width
    edge = gains[None, :] * jnp.exp(step_back[:, None] * pole_rates[None, :])
    decay = jnp.exp(-width * pole_rates)[:, None]
    partial = plain_finish(finish_info, totals, edge, decay, length)
    received = []
    for r in range(per):
        result = plain_combine([partial[r], *[shift_of(partial[w * per + r], ways, w, 0) for w in range(1, ways)]])
        pairs = []
        for c in range(count):
            for g in range(groups):
                m = (r + c % per_grp * 2 + g % 2) % per
                goal = ways * m + (g // 2 + c) % ways
                pairs.append((c * groups + g, goal * groups + c // per_grp))
        received.append(lax.ppermute(result, ("ctx", "grp"), pairs))
    return plain_arrange(lanes_info, received)


def spread(count, pairs, order, offsets):
    rand, best = random.Random(1), None

    def cost(flips):
        loads = {}
        for c in range(count):
            for r, pair in enumerate(pairs):
                for way in range(2):
                    goal = order[(order.index(c) + offsets[pair[way ^ flips[c][r]]]) % count]
                    lo, hi = sorted((c // 2, goal // 2))
                    keys = [(z, c % 2, way, goal > c) for z in range(lo, hi)]
                    if way != 2 * c // count:
                        keys.append((goal // 2, c % 2, way))
                    for key in keys:
                        loads[key] = loads.get(key, 0) + 1
        return max(loads.values()), sum(v * v for v in loads.values())

    for _ in range(20):
        flips = [[rand.randint(0, 1) for _ in pairs] for _ in range(count)]
        now, better = cost(flips), True
        while better:
            better = False
            for c in range(count):
                for r in range(len(pairs)):
                    flips[c][r] ^= 1
                    new = cost(flips)
                    if new < now:
                        now, better = new, True
                    else:
                        flips[c][r] ^= 1
        if best is None or now < best[0]:
            best = now, flips
    return best[1]


def final_rounds(count, groups):
    order, offsets = ring_of(count)
    if groups != 4 or count != 2 * groups:
        return None
    twos = [(s, s + 1) for s in range(1, count - 1, 2)] + [(0, count - 1)]
    pairs = twos[0::2] + twos[1::2]
    flips = spread(count, pairs, order, offsets)
    rounds = []
    for first in range(0, len(pairs), 2):
        for t in range(2):
            moves = []
            for c in range(count):
                for g in range(groups):
                    r = first + (t + g % 2) % 2
                    slot = pairs[r][g // 2 ^ flips[c][r]]
                    goal = order[(order.index(c) + offsets[slot]) % count]
                    moves.append((c * groups + g, goal * groups + c * groups // count))
            if len({b for _, b in moves}) != len(moves):
                return None
            rounds.append(moves)
    return pairs, flips, rounds


def per_device(out_grad, filter_mats, coeffs, pole_rates):
    count, groups = lax.axis_size("ctx"), lax.axis_size("grp")
    own_filters, features, _ = filter_mats.shape
    length, wide = out_grad.shape
    half, width = features // 2, length // 4
    tiled = half % 128 == 0 and wide % 128 == 0 and width % 128 == 0 and pole_rates.shape[0] % 16 == 0
    found = final_rounds(count, groups)
    if not tiled or own_filters % 2 or found is None:
        return plain_device(out_grad, filter_mats, coeffs, pole_rates)
    pairs, flips, rounds = found
    ways, per_grp = groups // 2, count // groups
    order, offsets = ring_of(count)
    right = [(order[i], order[(i + 1) % count]) for i in range(count)]
    left = [(b, a) for a, b in right]
    to = [(1, 0), (1, 1), (0, 1), (0, 0)]
    sources = [(0, 1), (0, 0), (1, 0), (1, 1)]

    def numbers(ctx, grp):
        way, here, at = grp // 2, grp % 2, order.index(ctx)
        firsts = [((way ^ w) * 2 + (here ^ h)) * (own_filters // 2) for w, h in sources]
        slots = [order[(at + o) % count] for o in offsets]
        second = [way ^ flip for flip in flips[ctx]]
        use = [slots[p[t]] for p, t in zip(pairs, second)] + [slots[p[1 - t]] for p, t in zip(pairs, second)]
        senders = [next(a for a, b in moves if b == ctx * groups + grp) for moves in rounds]
        lanes = [a // groups % per_grp * 2 + a % 2 for a in senders]
        return [[here], second, firsts, slots, use, lanes]

    row, (core_at, second_at, firsts_at, slots_at, use_at, lanes_at), _ = my_row(count, groups, numbers)
    swap = lambda x: shift_of(x, ways, 0, 1)
    together = lambda *x: lax.optimization_barrier(x)

    pieces = cut(filter_mats, to[:1], half, 2 * wide)
    gains = jnp.sqrt(-jnp.expm1(-2.0 * pole_rates))
    table = tables(coeffs, pole_rates, gains, width)
    mats = [None, None, shift_of(pieces[0], ways, *to[0])]
    going_right, going_left = out_grad, out_grad
    mine, other, totals = [out_grad], [swap(out_grad)], [None] * count
    back = lambda n: gains[None, :] * jnp.exp((jnp.arange(n, dtype=f32) - n)[:, None] * pole_rates[None, :])
    ahead = lambda n: jnp.exp(-n * pole_rates)[:, None]
    ends, far_ends = (back(width), ahead(width)), (back(length), ahead(length))

    def run(slots, use, closing=None):
        chosen = sorted({n for s in slots for n in use[s]})
        info_at = [core_at] + [firsts_at + n for n in chosen]
        work = [(chosen.index(n), b) for n in chosen for b, s in enumerate(slots) if n in use[s]]
        got = add_blocks(
            row, info_at, [mine[s] for s in slots], [other[s] for s in slots], [mats[n] for n in chosen], table,
            [totals[s] for s in slots], work, *(() if closing is None else (ends, second_at + closing)),
        )
        if closing is not None:
            return got
        for s, t in zip(slots, got):
            totals[s] = t

    for step in range(1, count // 2 + 1):
        arrived = [0] if step == 1 else [2 * step - 3, 2 * step - 2]
        if step > 1:
            other += [swap(mine[s]) for s in arrived]
        if step < count // 2:
            coming = [lax.ppermute(going_right, "ctx", right), lax.ppermute(going_left, "ctx", left)]
        else:
            coming = [
                lax.ppermute(going_right[: length // 2], "ctx", right),
                lax.ppermute(going_left[length // 2 :], "ctx", left),
            ]
        if step == 3:
            piece, mats[2] = together(pieces[1], mats[2])
            mats.append(shift_of(piece, ways, *to[1]))
        if step == 2:
            pieces += cut(filter_mats, to[1:], half, 2 * wide)
            mats[:2] = [swap(pieces[2]), pieces[3]]
        elif step > 2:
            slots = ([0] if step == 3 else []) + [2 * step - 5, 2 * step - 4]
            run(slots, {s: [0, 1, 2] for s in slots})
        done = [s for s in range(count) if totals[s] is not None]
        coming, swapped, table, sums, early, filter_mats = together(
            coming, other[-len(arrived) :], table, [totals[s] for s in done], mats[:3] if step > 1 else [], filter_mats
        )
        other[-len(arrived) :] = swapped
        mats[: len(early)] = early
        for s, t in zip(done, sums):
            totals[s] = t
        if step < count // 2:
            going_right, going_left = coming
            mine += coming
        else:
            mine.append(jnp.concatenate(coming))
    other.append(swap(mine[-1]))

    kept, sent, states = [None] * len(pairs), [None] * len(pairs), [None] * count
    for pair in [*sorted(pairs)[1:], sorted(pairs)[0]]:
        use = {s: [n for n in range(4) if totals[s] is None or n == 3] for s in pair}
        keep, send, *state = run(list(pair), use, pairs.index(pair))
        for s, st in zip(pair, state):
            states[s] = st
        kept[pairs.index(pair)], sent[pairs.index(pair)] = keep, send
    carry_kept, carry_sent = carry(row, slots_at, use_at, states, far_ends[1])
    sent[-1], carry_sent = together(sent[-1], carry_sent)
    carries = [carry_kept, shift_of(carry_sent, ways, 1, 0)]
    arrived = [shift_of(x, ways, 1, 0) for x in sent]
    received = []
    for first in range(0, len(pairs), 2):
        both = [first, first + 1]
        got = results(row, core_at, both, [kept[r] for r in both], [arrived[r] for r in both], carries, far_ends[0])
        received += [lax.ppermute(v, ("ctx", "grp"), moves) for v, moves in zip(got, rounds[first : first + 2])]
    return arrange(row, lanes_at, received)


def solution(mesh):
    placed = (P("ctx", "grp"), P("grp", "ctx", None), P(), P())
    return jax.shard_map(
        per_device, mesh=mesh, in_specs=placed, out_specs=P("ctx", "grp"), check_vma=False
    )
```

```python
import functools
import random

import jax
import jax.numpy as jnp
import numpy as np
from jax import lax
from jax.experimental import pallas as pl
from jax.experimental.pallas import tpu as pltpu
from jax.sharding import PartitionSpec as P

exact_prec = lax.Precision.HIGHEST
f32, bf16 = jnp.float32, jnp.bfloat16
NT = (((1,), (1,)), ((), ()))
VM = pl.BlockSpec(memory_space=pltpu.VMEM)
ANY = pl.BlockSpec(memory_space=pl.ANY)
SM = pl.BlockSpec(memory_space=pltpu.SMEM)


def params(mib=16):
    return pltpu.CompilerParams(vmem_limit_bytes=mib * 2**20)


def split2(x):
    high = x.astype(bf16)
    return high, (x - high.astype(f32)).astype(bf16)


def tables_kernel(poles_ref, out):
    poles, width = poles_ref.shape[0], out.shape[2] // 4
    rate, gain = poles_ref[:, 0:1], poles_ref[:, 1:2]
    lag = lax.broadcasted_iota(jnp.int32, (poles, width), 1).astype(f32)
    decay = jnp.exp(-rate * lag)
    gained = gain * decay
    columns = lax.broadcasted_iota(jnp.int32, (poles, poles_ref.shape[1]), 1)

    @pl.loop(0, out.shape[0])
    def _(pair):
        for j in range(2):
            chosen = jnp.where(columns == 2 + 2 * pair + j, poles_ref[...], 0.0)
            coef = jnp.sum(chosen, axis=1, keepdims=True)
            phi = jnp.sum(coef * gained, axis=0, keepdims=True)
            line = jnp.concatenate([phi, jnp.zeros((1, width), f32)], axis=1)
            rolled = pltpu.roll(jnp.broadcast_to(line, (width, 2 * width)), 0, 1, stride=1, stride_axis=0)
            near, weight = split2(rolled[:, :width]), split2(coef * decay)
            for at in range(2):
                lanes = slice((2 * at + j) * width, (2 * at + j + 1) * width)
                out[pair, :width, lanes] = near[at]
                out[pair, width:, lanes] = weight[at]


def tables(coeffs, rates, gains, width):
    filters, poles = coeffs.shape
    joined = jnp.concatenate([rates[:, None], gains[:, None], coeffs.T], axis=1)
    return pl.pallas_call(
        tables_kernel,
        in_specs=[VM],
        out_specs=VM,
        out_shape=jax.ShapeDtypeStruct((filters // 2, width + poles, 4 * width), bf16),
        compiler_params=params(),
        cost_estimate=pl.CostEstimate(flops=int(4e9), bytes_accessed=0, transcendentals=0),
        name="pole_tables",
    )(joined)


def cut_kernel(to, mats, *refs):
    outs, sems = refs[:-1], refs[-1]
    way, here = lax.axis_index("grp") // 2, lax.axis_index("grp") % 2
    copies = []
    for i, (by_way, by_core, lo, n) in enumerate(to):
        _, half, cols = outs[i].shape
        row = (1 - here if by_core else here) * half
        col = (1 - way if by_way else way) * cols
        src = mats.at[pl.ds(lo, n), pl.ds(pl.multiple_of(row, half), half), pl.ds(pl.multiple_of(col, cols), cols)]
        copies.append(pltpu.make_async_copy(src, outs[i], sems.at[i]))
    for c in copies:
        c.start()
    for c in copies:
        c.wait()


def cut(mats, to, half, cols):
    return pl.pallas_call(
        functools.partial(cut_kernel, to),
        in_specs=[ANY],
        out_specs=[VM] * len(to),
        out_shape=[jax.ShapeDtypeStruct((n, half, cols), bf16) for *_, n in to],
        scratch_shapes=[pltpu.SemaphoreType.DMA((len(to),))],
        compiler_params=params(60),
        name="cut_filters",
    )(mats)


def products(work, info_at, info, mine, other, mats, table, before, after, held):
    wide = mine[0].shape[1]
    here = info[info_at[0]]
    width = table.shape[2] // 4
    half = mats[0].shape[1]
    subs = mine[0].shape[0] // width
    units = [(i, n, b) for n, b in work for i in range(mats[n].shape[0] // 2)]
    for u, (i, n, b) in enumerate(units):
        two = mats[n].at[pl.ds(2 * i, 2)]
        m_mine = two[:, :, pl.ds(pl.multiple_of(here * wide, wide), wide)].reshape(2 * half, wide)
        m_other = two[:, :, pl.ds(pl.multiple_of((1 - here) * wide, wide), wide)].reshape(2 * half, wide)
        proj = lax.dot_general(mine[b][...], m_mine, NT, preferred_element_type=f32)
        proj += lax.dot_general(other[b][...], m_other, NT, preferred_element_type=f32)
        for at, part in enumerate(split2(proj)):
            for j in range(2):
                rows = pl.ds((2 * at + j) * width, width)
                for s in range(subs):
                    held[u, rows, s * half : (s + 1) * half] = part[
                        s * width : (s + 1) * width, j * half : (j + 1) * half
                    ]
    begun = set()
    for u, (i, n, b) in enumerate(units):
        pair = info[info_at[1 + n]] + i
        high, low = held[u, : 2 * width, :], held[u, 2 * width :, :]
        add = jnp.dot(table[pair, :, : 2 * width], high, preferred_element_type=f32)
        add += jnp.dot(table[pair, :, 2 * width :], high, preferred_element_type=f32)
        add += jnp.dot(table[pair, :, : 2 * width], low, preferred_element_type=f32)
        if b in begun:
            after[b][...] += add
        else:
            after[b][...] = add if before[b] is None else before[b][...] + add
            begun.add(b)


def blocks_kernel(blocks, sets, work, info_at, fresh, closing, splits, info, *refs):
    refs = list(refs)
    take = lambda n: [refs.pop(0) for _ in range(n)]
    mine, other, mats, (table,) = take(blocks), take(blocks), take(sets), take(1)
    before = [None if new else refs.pop(0) for new in fresh]
    if not closing:
        after, (held,) = take(blocks), take(1)
        products(work, info_at, info, mine, other, mats, table, before, after, held)
        return
    edge, decay, kept, *sent = take(3 + splits)
    states = take(blocks)
    held, after = refs
    after = [after.at[b] for b in range(blocks)]
    products(work, info_at, info, mine, other, mats, table, before, after, held)
    width, poles = edge.shape
    half = mats[0].shape[1]
    subs = mine[0].shape[0] // width
    eh, el = split2(edge[...])
    left = jnp.concatenate([eh, el, eh], axis=1)
    values = []
    for b in range(blocks):
        state, enters, carried = after[b][width:, :], [], jnp.zeros((poles, half), f32)
        for s in reversed(range(subs)):
            enters.append(carried)
            carried = state[:, s * half : (s + 1) * half] + decay[...] * carried
        states[b][...] = carried
        ch, cl = split2(jnp.concatenate(enters[::-1], axis=1))
        far = jnp.dot(left, jnp.concatenate([ch, ch, cl], axis=0), preferred_element_type=f32)
        values.append(after[b][:width, :] + far)
    first = info[closing] == 0
    rows = sent[0].shape[0]
    for s in range(subs):
        lanes, at = slice(s * half, (s + 1) * half), s * width
        one, two = [value[:, lanes] for value in values]
        kept[at : at + width, :] = jnp.where(first, one, two)
        sent[at // rows][at % rows : at % rows + width, :] = jnp.where(first, two, one)


def add_blocks(info, info_at, mine, other, mats, table, totals, work, ends=None, closing=0, splits=1):
    blocks, sets = len(mine), len(mats)
    fresh = [t is None for t in totals]
    old = [t for t in totals if t is not None]
    half, length = mats[0].shape[1], mine[0].shape[0]
    height, tw = table.shape[1:]
    lanes = length // (tw // 4) * half
    units = sum(mats[n].shape[0] // 2 for n, _ in work)
    first = 1 + 2 * blocks + sets + 1
    scratch = [pltpu.VMEM((units, tw, lanes), bf16)]
    if ends is None:
        ends, aliases = (), {first + i: b for i, b in enumerate(b for b in range(blocks) if not fresh[b])}
        shapes = [jax.ShapeDtypeStruct((height, lanes), f32)] * blocks
    else:
        aliases = {}
        shapes = [jax.ShapeDtypeStruct((length, half), f32)]
        shapes += [jax.ShapeDtypeStruct((length // splits, half), f32)] * splits
        shapes += [jax.ShapeDtypeStruct((height - tw // 4, half), f32)] * blocks
        scratch.append(pltpu.VMEM((blocks, height, lanes), f32))
    return pl.pallas_call(
        functools.partial(blocks_kernel, blocks, sets, work, info_at, fresh, closing, splits),
        in_specs=[SM] + [VM] * (2 * blocks + sets + 1 + len(old) + len(ends)),
        out_specs=[VM] * len(shapes),
        out_shape=shapes,
        scratch_shapes=scratch,
        input_output_aliases=aliases,
        compiler_params=params(24 if closing else 16),
        cost_estimate=pl.CostEstimate(flops=int(units * 0.6e9), bytes_accessed=0, transcendentals=0),
        name="close_blocks" if closing else "add_blocks",
    )(info, *mine, *other, *mats, table, *old, *ends)


def carry_kernel(count, slots_at, use_at, info, *refs):
    states, decay, (kept, sent), (held, entering) = refs[:count], refs[count], refs[count + 1 : count + 3], refs[count + 3 :]
    for s in range(count):
        held[info[slots_at + s]] = states[s][...]
    carried = jnp.zeros_like(states[0])
    for c in reversed(range(count)):
        entering[c] = carried
        carried = held[c] + decay[...] * carried
    per = kept.shape[0]
    for r in range(per):
        kept[r] = entering[info[use_at + r]]
        sent[r] = entering[info[use_at + per + r]]


def carry(info, slots_at, use_at, states, decay):
    count, shape = len(states), states[0].shape
    return pl.pallas_call(
        functools.partial(carry_kernel, count, slots_at, use_at),
        in_specs=[SM] + [VM] * (count + 1),
        out_specs=[VM] * 2,
        out_shape=[jax.ShapeDtypeStruct((count // 2, *shape), f32)] * 2,
        scratch_shapes=[pltpu.VMEM((count, *shape), f32)] * 2,
        compiler_params=params(),
        name="carry_states",
    )(info, *states, decay)


def result_kernel(pairs, splits, here_at, info, *refs):
    refs = list(refs)
    take = lambda n: [refs.pop(0) for _ in range(n)]
    kept, arrived = take(len(pairs)), [take(n) for n in splits]
    carry_kept, carry_arrived, edge, *outs = refs
    eh, el = split2(edge[...])
    left = jnp.concatenate([eh, el, eh], axis=1)
    values = []
    for n, r in enumerate(pairs):
        ch, cl = split2(carry_kept[r] + carry_arrived[r])
        far = jnp.dot(left, jnp.concatenate([ch, ch, cl], axis=0), preferred_element_type=f32)
        other = jnp.concatenate([part[...] for part in arrived[n]], axis=0)
        values.append((kept[n][...] + other + far).astype(bf16))
    first = info[here_at] == 0
    outs[0][...] = jnp.where(first, values[0], values[1])
    outs[1][...] = jnp.where(first, values[1], values[0])


def results(info, here_at, pairs, kept, arrived, carries, edge):
    return pl.pallas_call(
        functools.partial(result_kernel, pairs, [len(parts) for parts in arrived], here_at),
        in_specs=[SM] + [VM] * (len(pairs) + sum(len(parts) for parts in arrived) + 3),
        out_specs=[VM] * len(pairs),
        out_shape=[jax.ShapeDtypeStruct(kept[0].shape, bf16)] * len(pairs),
        compiler_params=params(),
        name="finish_blocks",
    )(info, *kept, *[part for parts in arrived for part in parts], *carries, edge)


def arrange_kernel(count, lanes_at, info, *refs):
    out = refs[count]
    lanes = refs[0].shape[1]
    for r in range(count):
        out[:, pl.ds(pl.multiple_of(info[lanes_at + r] * lanes, lanes), lanes)] = refs[r][...]


def arrange(info, lanes_at, parts):
    rows, lanes = parts[0].shape
    return pl.pallas_call(
        functools.partial(arrange_kernel, len(parts), lanes_at),
        in_specs=[SM] + [VM] * len(parts),
        out_specs=VM,
        out_shape=jax.ShapeDtypeStruct((rows, lanes * len(parts)), bf16),
        compiler_params=params(),
        name="arrange_features",
    )(info, *parts)


def plain_tables(coeffs, rates, gains, width):
    lag = jnp.arange(width, dtype=f32)
    decay = jnp.exp(-rates[:, None] * lag[None, :])
    shift = lag[None, :] - lag[:, None]
    phi = jnp.dot(coeffs * gains[None, :], decay, precision=exact_prec)
    near = jnp.where(shift >= 0, phi[:, jnp.maximum(shift, 0).astype(jnp.int32)], 0.0)
    return jnp.concatenate([near, coeffs[:, :, None] * decay[None]], axis=1)


def plain_cut(mats, info, plan, half, cols):
    return [
        lax.dynamic_slice(mats, (lo, info[2 * i], info[2 * i + 1]), (n, half, cols)) for i, (lo, n) in enumerate(plan)
    ]


def plain_add(info, mine, other, mats, table, totals, work):
    results = []
    wide, width = mine[0].shape[1], table.shape[2]
    for b in range(len(mine)):
        rows = jnp.concatenate([mine[b], other[b]], axis=1)
        total = 0.0 if totals[b] is None else totals[b]
        for n in [n for n, at in work if at == b]:
            use = lax.dynamic_slice_in_dim(table, 2 * info[1 + n], mats[n].shape[0], 0)
            swapped = jnp.where(info[0] == 0, mats[n], jnp.roll(mats[n], wide, axis=2))
            proj = jnp.einsum("tj,kij->kti", rows, swapped, preferred_element_type=f32)
            proj = jnp.concatenate(jnp.split(proj, rows.shape[0] // width, axis=1), axis=2)
            total = total + jnp.einsum("kst,kti->si", use, proj, precision=exact_prec)
        results.append(total)
    return results


def plain_finish(info, totals, edge, decay, length):
    count, width = len(totals), edge.shape[0]
    subs = length // width
    held = jnp.zeros((count,) + totals[0].shape, f32)
    for s in range(count):
        held = lax.dynamic_update_slice(held, totals[s][None], (info[s], 0, 0))
    carried, values = jnp.zeros((edge.shape[1], totals[0].shape[1] // subs), f32), [None] * count
    for c in reversed(range(count)):
        enters = []
        for state in reversed(jnp.split(held[c, width:], subs, axis=1)):
            enters.append(carried)
            carried = state + decay * carried
        far = jnp.dot(edge, jnp.concatenate(enters[::-1], axis=1), precision=exact_prec)
        values[c] = jnp.concatenate(jnp.split(held[c, :width] + far, subs, axis=1), axis=0)
    values = jnp.stack(values)
    return [values[info[count + n]] for n in range(count)]


def plain_combine(parts):
    return sum(parts[1:], parts[0]).astype(bf16)


def plain_arrange(info, parts):
    rows, lanes = parts[0].shape
    out = jnp.zeros((rows, lanes * len(parts)), bf16)
    for r, part in enumerate(parts):
        out = lax.dynamic_update_slice(out, part, (0, info[r] * lanes))
    return out


def ring_of(count):
    order = [*range(0, count, 2), *reversed(range(1, count, 2))]
    offsets = [0]
    for step in range(1, count // 2):
        offsets += [-step, step]
    return order, [*offsets, count // 2]


def shift_of(x, ways, by_way, by_core):
    rank = lambda w, h: (w % ways) * 2 + h
    return lax.ppermute(x, "grp", [(rank(w, h), rank(w + by_way, h ^ by_core)) for w in range(ways) for h in range(2)])


def my_row(count, groups, numbers):
    rows = [numbers(c, g) for c in range(count) for g in range(groups)]
    ends = np.cumsum([len(part) for part in rows[0]])
    known = jnp.asarray(np.array([sum(r, []) for r in rows], np.int32))
    me = lax.axis_index("ctx") * groups + lax.axis_index("grp")
    row = lax.dynamic_slice(known, (me, 0), (1, known.shape[1]))[0]
    return row, [int(e) - len(part) for e, part in zip(ends, rows[0])], [int(e) for e in ends]


def plain_device(out_grad, filter_mats, coeffs, pole_rates):
    count, groups = lax.axis_size("ctx"), lax.axis_size("grp")
    ways, per_grp = groups // 2, count // groups
    per = count // ways
    own_filters, features, _ = filter_mats.shape
    length, wide = out_grad.shape
    half, width = features // 2, length // 4
    order, offsets = ring_of(count)
    right = [(order[i], order[(i + 1) % count]) for i in range(count)]
    left = [(b, a) for a, b in right]
    to = [(w, h) for w in range(1, ways) for h in range(2)] + [(0, 1), (0, 0)]
    plan = [(0, own_filters)] * len(to)

    def numbers(ctx, grp):
        way, here, at = grp // 2, grp % 2, order.index(ctx)
        cuts = []
        for w, h in to:
            cuts += [(here ^ h) * half, (way + w) % ways * 2 * wide]
        firsts = [(((way - w) % ways) * 2 + (here ^ h)) * (own_filters // 2) for w, h in to]
        turn = ctx % per_grp * 2 + here
        slots = [order[(at + o) % count] for o in offsets]
        use = [ways * ((r + turn) % per) + (way + w + ctx) % ways for w in range(ways) for r in range(per)]
        return [cuts, [here] + firsts, slots + use, [(ctx // ways - r) % per for r in range(per)]]

    row, begins, ends = my_row(count, groups, numbers)
    cuts, firsts, finish_info, lanes_info = [row[b:e] for b, e in zip(begins, ends)]
    swap = lambda x: shift_of(x, ways, 0, 1)
    mine, other = [out_grad], [swap(out_grad)]
    going_right, going_left = out_grad, out_grad
    for step in range(1, count // 2):
        going_right = lax.ppermute(going_right, "ctx", right)
        going_left = lax.ppermute(going_left, "ctx", left)
        mine += [going_right, going_left]
        other += [swap(going_right), swap(going_left)]
    mine.append(lax.ppermute(going_right, "ctx", right))
    other.append(swap(mine[-1]))
    pieces = plain_cut(filter_mats, cuts, plan, half, 2 * wide)
    mats = [shift_of(p, ways, w, h) for p, (w, h) in zip(pieces[:-1], to[:-1])] + pieces[-1:]
    gains = jnp.sqrt(-jnp.expm1(-2.0 * pole_rates))
    table = plain_tables(coeffs, pole_rates, gains, width)
    work = [(n, 0) for n in range(len(mats))]
    totals = [plain_add(firsts, [m], [o], mats, table, [None], work)[0] for m, o in zip(mine, other)]
    step_back = jnp.arange(width, dtype=f32) - width
    edge = gains[None, :] * jnp.exp(step_back[:, None] * pole_rates[None, :])
    decay = jnp.exp(-width * pole_rates)[:, None]
    partial = plain_finish(finish_info, totals, edge, decay, length)
    received = []
    for r in range(per):
        result = plain_combine([partial[r], *[shift_of(partial[w * per + r], ways, w, 0) for w in range(1, ways)]])
        pairs = []
        for c in range(count):
            for g in range(groups):
                m = (r + c % per_grp * 2 + g % 2) % per
                goal = ways * m + (g // 2 + c) % ways
                pairs.append((c * groups + g, goal * groups + c // per_grp))
        received.append(lax.ppermute(result, ("ctx", "grp"), pairs))
    return plain_arrange(lanes_info, received)


def spread(count, pairs, order, offsets):
    rand, best = random.Random(1), None

    def cost(flips):
        loads = {}
        for c in range(count):
            for r, pair in enumerate(pairs):
                for way in range(2):
                    goal = order[(order.index(c) + offsets[pair[way ^ flips[c][r]]]) % count]
                    lo, hi = sorted((c // 2, goal // 2))
                    keys = [(z, c % 2, way, goal > c) for z in range(lo, hi)]
                    if way != 2 * c // count:
                        keys.append((goal // 2, c % 2, way))
                    for key in keys:
                        loads[key] = loads.get(key, 0) + 1
        return max(loads.values()), sum(v * v for v in loads.values())

    for _ in range(20):
        flips = [[rand.randint(0, 1) for _ in pairs] for _ in range(count)]
        now, better = cost(flips), True
        while better:
            better = False
            for c in range(count):
                for r in range(len(pairs)):
                    flips[c][r] ^= 1
                    new = cost(flips)
                    if new < now:
                        now, better = new, True
                    else:
                        flips[c][r] ^= 1
        if best is None or now < best[0]:
            best = now, flips
    return best[1]


def final_rounds(count, groups):
    order, offsets = ring_of(count)
    if groups != 4 or count != 2 * groups:
        return None
    twos = [(s, s + 1) for s in range(1, count - 1, 2)] + [(0, count - 1)]
    pairs = twos[0::2] + twos[1::2]
    flips = spread(count, pairs, order, offsets)
    rounds = []
    for first in range(0, len(pairs), 2):
        for t in range(2):
            moves = []
            for c in range(count):
                for g in range(groups):
                    r = first + (t + g % 2) % 2
                    slot = pairs[r][g // 2 ^ flips[c][r]]
                    goal = order[(order.index(c) + offsets[slot]) % count]
                    moves.append((c * groups + g, goal * groups + c * groups // count))
            if len({b for _, b in moves}) != len(moves):
                return None
            rounds.append(moves)
    return pairs, flips, rounds


def per_device(out_grad, filter_mats, coeffs, pole_rates):
    count, groups = lax.axis_size("ctx"), lax.axis_size("grp")
    own_filters, features, _ = filter_mats.shape
    length, wide = out_grad.shape
    half, width = features // 2, length // 4
    tiled = half % 128 == 0 and wide % 128 == 0 and width % 128 == 0 and pole_rates.shape[0] % 16 == 0
    found = final_rounds(count, groups)
    if not tiled or own_filters % 4 or found is None:
        return plain_device(out_grad, filter_mats, coeffs, pole_rates)
    pairs, flips, rounds = found
    ways, per_grp = groups // 2, count // groups
    order, offsets = ring_of(count)
    right = [(order[i], order[(i + 1) % count]) for i in range(count)]
    left = [(b, a) for a, b in right]
    some = own_filters // 2
    far_to = [(1, h, 0, own_filters) for h in range(2)]
    swap_to = [(0, 1, lo, some) for lo in (0, some)]
    own_to = (0, 0, 0, own_filters)

    def numbers(ctx, grp):
        way, here, at = grp // 2, grp % 2, order.index(ctx)
        firsts = [(((way ^ w) * 2 + (here ^ h)) * own_filters + lo) // 2 for w, h, lo, _ in [*swap_to, own_to, *far_to]]
        slots = [order[(at + o) % count] for o in offsets]
        second = [way ^ flip for flip in flips[ctx]]
        use = [slots[p[t]] for p, t in zip(pairs, second)] + [slots[p[1 - t]] for p, t in zip(pairs, second)]
        senders = [next(a for a, b in moves if b == ctx * groups + grp) for moves in rounds]
        lanes = [a // groups % per_grp * 2 + a % 2 for a in senders]
        return [[here], second, firsts, slots, use, lanes]

    row, (core_at, second_at, firsts_at, slots_at, use_at, lanes_at), _ = my_row(count, groups, numbers)
    swap = lambda x: shift_of(x, ways, 0, 1)
    together = lambda *x: lax.optimization_barrier(x)

    pieces = cut(filter_mats, far_to[:1], half, 2 * wide)
    gains = jnp.sqrt(-jnp.expm1(-2.0 * pole_rates))
    table = ()
    cut_early = cut(filter_mats, [*swap_to, own_to, far_to[1]], half, 2 * wide)
    mats = [None, None, None, shift_of(pieces[0], ways, *far_to[0][:2])]
    going_right, going_left = out_grad, out_grad
    mine, other, totals = [out_grad], [swap(out_grad)], [None] * count
    back = lambda n: gains[None, :] * jnp.exp((jnp.arange(n, dtype=f32) - n)[:, None] * pole_rates[None, :])
    ahead = lambda n: jnp.exp(-n * pole_rates)[:, None]
    ends, far_ends = (back(width), ahead(width)), (back(length), ahead(length))

    done_sets, splits = {}, [1] * (len(pairs) - 1) + [2]

    def run(slots, use, closing=None):
        for s in slots:
            done_sets.setdefault(s, set()).update(use[s])
        chosen = sorted({n for s in slots for n in use[s]})
        info_at = [core_at] + [firsts_at + n for n in chosen]
        work = [(chosen.index(n), b) for n in chosen for b, s in enumerate(slots) if n in use[s]]
        got = add_blocks(
            row, info_at, [mine[s] for s in slots], [other[s] for s in slots], [mats[n] for n in chosen], table,
            [totals[s] for s in slots], work, *(() if closing is None else (ends, second_at + closing, splits[closing])),
        )
        if closing is not None:
            return got
        for s, t in zip(slots, got):
            totals[s] = t

    for step in range(1, count // 2 + 1):
        arrived = [0] if step == 1 else [2 * step - 3, 2 * step - 2]
        if step > 1:
            other += [swap(mine[s]) for s in arrived]
        if step < count // 2:
            coming = [lax.ppermute(going_right, "ctx", right), lax.ppermute(going_left, "ctx", left)]
        else:
            coming = [
                lax.ppermute(going_right[: length // 2], "ctx", right),
                lax.ppermute(going_left[length // 2 :], "ctx", left),
            ]
        if step == 3:
            piece, mats[3] = together(next_piece, mats[3])
            mats.append(shift_of(piece, ways, *far_to[1][:2]))
        if step == 2:
            table = tables(coeffs, later_rates, gains, width)
            mats[:2] = [swap(p) for p in pieces[:2]]
            mats[2], next_piece = pieces[2:]
        elif step > 2:
            slots = ([0] if step == 3 else []) + [2 * step - 5, 2 * step - 4]
            run(slots, {s: [0, 1, 2, 3] for s in slots})
        if step == count // 2:
            slots = [2 * step - 3, 2 * step - 2]
            run(slots, {s: [2] for s in slots})
        done = [s for s in range(count) if totals[s] is not None]
        coming, swapped, table, sums, early, filter_mats, cut_early = together(
            coming, other[-len(arrived) :], table, [totals[s] for s in done], mats[:4] if step > 1 else [], filter_mats, cut_early
        )
        if step == 1:
            pieces, row, coming = together(cut_early, row, coming)
        if step == 1:
            later_rates, coming = together(pole_rates, coming)
        other[-len(arrived) :] = swapped
        mats[: len(early)] = early
        for s, t in zip(done, sums):
            totals[s] = t
        if step < count // 2:
            going_right, going_left = coming
            mine += coming
        else:
            mine.append(jnp.concatenate(coming))
    other.append(swap(mine[-1]))

    kept, sent, states = [None] * len(pairs), [None] * len(pairs), [None] * count
    for pair in [*sorted(pairs)[1:], sorted(pairs)[0]]:
        use = {s: [n for n in range(5) if n not in done_sets.get(s, ())] for s in pair}
        keep, *send = run(list(pair), use, pairs.index(pair))
        send, state = send[:-2], send[-2:]
        for s, st in zip(pair, state):
            states[s] = st
        kept[pairs.index(pair)], sent[pairs.index(pair)] = keep, send
    carry_kept, carry_sent = carry(row, slots_at, use_at, states, far_ends[1])
    carries = [carry_kept, shift_of(carry_sent, ways, 1, 0)]
    arrived = [[shift_of(x, ways, 1, 0) for x in parts] for parts in sent]
    received = []
    for first in range(0, len(pairs), 2):
        both = [first, first + 1]
        got = results(row, core_at, both, [kept[r] for r in both], [arrived[r] for r in both], carries, far_ends[0])
        received += [lax.ppermute(v, ("ctx", "grp"), moves) for v, moves in zip(got, rounds[first : first + 2])]
    return arrange(row, lanes_at, received)


def solution(mesh):
    placed = (P("ctx", "grp"), P("grp", "ctx", None), P(), P())
    return jax.shard_map(
        per_device, mesh=mesh, in_specs=placed, out_specs=P("ctx", "grp"), check_vma=False
    )
```

```python
import functools
import random

import jax
import jax.numpy as jnp
import numpy as np
from jax import lax
from jax.experimental import pallas as pl
from jax.experimental.pallas import tpu as pltpu
from jax.sharding import PartitionSpec as P

exact_prec = lax.Precision.HIGHEST
f32, bf16 = jnp.float32, jnp.bfloat16
NT = (((1,), (1,)), ((), ()))
VM = pl.BlockSpec(memory_space=pltpu.VMEM)
ANY = pl.BlockSpec(memory_space=pl.ANY)
SM = pl.BlockSpec(memory_space=pltpu.SMEM)


def params(mib=16):
    return pltpu.CompilerParams(vmem_limit_bytes=mib * 2**20)


def split2(x):
    high = x.astype(bf16)
    return high, (x - high.astype(f32)).astype(bf16)


def tables_kernel(poles_ref, out):
    poles, width = poles_ref.shape[0], out.shape[2] // 4
    rate, gain = poles_ref[:, 0:1], poles_ref[:, 1:2]
    lag = lax.broadcasted_iota(jnp.int32, (poles, width), 1).astype(f32)
    decay = jnp.exp(-rate * lag)
    gained = gain * decay
    columns = lax.broadcasted_iota(jnp.int32, (poles, poles_ref.shape[1]), 1)

    @pl.loop(0, out.shape[0])
    def _(pair):
        for j in range(2):
            chosen = jnp.where(columns == 2 + 2 * pair + j, poles_ref[...], 0.0)
            coef = jnp.sum(chosen, axis=1, keepdims=True)
            phi = jnp.sum(coef * gained, axis=0, keepdims=True)
            line = jnp.concatenate([phi, jnp.zeros((1, width), f32)], axis=1)
            rolled = pltpu.roll(jnp.broadcast_to(line, (width, 2 * width)), 0, 1, stride=1, stride_axis=0)
            near, weight = split2(rolled[:, :width]), split2(coef * decay)
            for at in range(2):
                lanes = slice((2 * at + j) * width, (2 * at + j + 1) * width)
                out[pair, :width, lanes] = near[at]
                out[pair, width:, lanes] = weight[at]


def tables(coeffs, rates, gains, width):
    filters, poles = coeffs.shape
    joined = jnp.concatenate([rates[:, None], gains[:, None], coeffs.T], axis=1)
    return pl.pallas_call(
        tables_kernel,
        in_specs=[VM],
        out_specs=VM,
        out_shape=jax.ShapeDtypeStruct((filters // 2, width + poles, 4 * width), bf16),
        compiler_params=params(),
        cost_estimate=pl.CostEstimate(flops=int(4e9), bytes_accessed=0, transcendentals=0),
        name="pole_tables",
    )(joined)


def cut_kernel(to, mats, *refs):
    outs, sems = refs[:-1], refs[-1]
    way, here = lax.axis_index("grp") // 2, lax.axis_index("grp") % 2
    copies = []
    for i, (by_way, by_core, lo, n) in enumerate(to):
        _, half, cols = outs[i].shape
        row = (1 - here if by_core else here) * half
        col = (1 - way if by_way else way) * cols
        src = mats.at[pl.ds(lo, n), pl.ds(pl.multiple_of(row, half), half), pl.ds(pl.multiple_of(col, cols), cols)]
        copies.append(pltpu.make_async_copy(src, outs[i], sems.at[i]))
    for c in copies:
        c.start()
    for c in copies:
        c.wait()


def cut(mats, to, half, cols):
    return pl.pallas_call(
        functools.partial(cut_kernel, to),
        in_specs=[ANY],
        out_specs=[VM] * len(to),
        out_shape=[jax.ShapeDtypeStruct((n, half, cols), bf16) for *_, n in to],
        scratch_shapes=[pltpu.SemaphoreType.DMA((len(to),))],
        compiler_params=params(60),
        name="cut_filters",
    )(mats)


def products(work, info_at, info, mine, other, mats, table, before, after, held):
    wide = mine[0].shape[1]
    here = info[info_at[0]]
    width = table.shape[2] // 4
    half = mats[0].shape[1]
    subs = mine[0].shape[0] // width
    units = [(i, n, b) for n, b in work for i in range(mats[n].shape[0] // 2)]
    for u, (i, n, b) in enumerate(units):
        two = mats[n].at[pl.ds(2 * i, 2)]
        m_mine = two[:, :, pl.ds(pl.multiple_of(here * wide, wide), wide)].reshape(2 * half, wide)
        m_other = two[:, :, pl.ds(pl.multiple_of((1 - here) * wide, wide), wide)].reshape(2 * half, wide)
        proj = lax.dot_general(mine[b][...], m_mine, NT, preferred_element_type=f32)
        proj += lax.dot_general(other[b][...], m_other, NT, preferred_element_type=f32)
        for at, part in enumerate(split2(proj)):
            for j in range(2):
                rows = pl.ds((2 * at + j) * width, width)
                for s in range(subs):
                    held[u, rows, s * half : (s + 1) * half] = part[
                        s * width : (s + 1) * width, j * half : (j + 1) * half
                    ]
    begun = set()
    for u, (i, n, b) in enumerate(units):
        pair = info[info_at[1 + n]] + i
        high, low = held[u, : 2 * width, :], held[u, 2 * width :, :]
        add = jnp.dot(table[pair, :, : 2 * width], high, preferred_element_type=f32)
        add += jnp.dot(table[pair, :, 2 * width :], high, preferred_element_type=f32)
        add += jnp.dot(table[pair, :, : 2 * width], low, preferred_element_type=f32)
        if b in begun:
            after[b][...] += add
        else:
            after[b][...] = add if before[b] is None else before[b][...] + add
            begun.add(b)


def blocks_kernel(blocks, sets, work, info_at, fresh, closing, splits, info, *refs):
    refs = list(refs)
    take = lambda n: [refs.pop(0) for _ in range(n)]
    mine, other, mats, (table,) = take(blocks), take(blocks), take(sets), take(1)
    before = [None if new else refs.pop(0) for new in fresh]
    if not closing:
        after, (held,) = take(blocks), take(1)
        products(work, info_at, info, mine, other, mats, table, before, after, held)
        return
    edge, decay, kept, *sent = take(3 + splits)
    states = take(blocks)
    held, after = refs
    after = [after.at[b] for b in range(blocks)]
    products(work, info_at, info, mine, other, mats, table, before, after, held)
    width, poles = edge.shape
    half = mats[0].shape[1]
    subs = mine[0].shape[0] // width
    eh, el = split2(edge[...])
    left = jnp.concatenate([eh, el, eh], axis=1)
    values = []
    for b in range(blocks):
        state, enters, carried = after[b][width:, :], [], jnp.zeros((poles, half), f32)
        for s in reversed(range(subs)):
            enters.append(carried)
            carried = state[:, s * half : (s + 1) * half] + decay[...] * carried
        states[b][...] = carried
        ch, cl = split2(jnp.concatenate(enters[::-1], axis=1))
        far = jnp.dot(left, jnp.concatenate([ch, ch, cl], axis=0), preferred_element_type=f32)
        values.append(after[b][:width, :] + far)
    first = info[closing] == 0
    rows = sent[0].shape[0]
    for s in range(subs):
        lanes, at = slice(s * half, (s + 1) * half), s * width
        one, two = [value[:, lanes] for value in values]
        kept[at : at + width, :] = jnp.where(first, one, two)
        sent[at // rows][at % rows : at % rows + width, :] = jnp.where(first, two, one)


def add_blocks(info, info_at, mine, other, mats, table, totals, work, ends=None, closing=0, splits=1):
    blocks, sets = len(mine), len(mats)
    fresh = [t is None for t in totals]
    old = [t for t in totals if t is not None]
    half, length = mats[0].shape[1], mine[0].shape[0]
    height, tw = table.shape[1:]
    lanes = length // (tw // 4) * half
    units = sum(mats[n].shape[0] // 2 for n, _ in work)
    first = 1 + 2 * blocks + sets + 1
    scratch = [pltpu.VMEM((units, tw, lanes), bf16)]
    if ends is None:
        ends, aliases = (), {first + i: b for i, b in enumerate(b for b in range(blocks) if not fresh[b])}
        shapes = [jax.ShapeDtypeStruct((height, lanes), f32)] * blocks
    else:
        aliases = {}
        shapes = [jax.ShapeDtypeStruct((length, half), f32)]
        shapes += [jax.ShapeDtypeStruct((length // splits, half), f32)] * splits
        shapes += [jax.ShapeDtypeStruct((height - tw // 4, half), f32)] * blocks
        scratch.append(pltpu.VMEM((blocks, height, lanes), f32))
    return pl.pallas_call(
        functools.partial(blocks_kernel, blocks, sets, work, info_at, fresh, closing, splits),
        in_specs=[SM] + [VM] * (2 * blocks + sets + 1 + len(old) + len(ends)),
        out_specs=[VM] * len(shapes),
        out_shape=shapes,
        scratch_shapes=scratch,
        input_output_aliases=aliases,
        compiler_params=params(14),
        cost_estimate=pl.CostEstimate(flops=int(units * 0.6e9), bytes_accessed=0, transcendentals=0),
        name="close_blocks" if closing else "add_blocks",
    )(info, *mine, *other, *mats, table, *old, *ends)


def carry_kernel(count, slots_at, use_at, info, *refs):
    states, decay, (kept, sent), (held, entering) = refs[:count], refs[count], refs[count + 1 : count + 3], refs[count + 3 :]
    for s in range(count):
        held[info[slots_at + s]] = states[s][...]
    carried = jnp.zeros_like(states[0])
    for c in reversed(range(count)):
        entering[c] = carried
        carried = held[c] + decay[...] * carried
    per = kept.shape[0]
    for r in range(per):
        kept[r] = entering[info[use_at + r]]
        sent[r] = entering[info[use_at + per + r]]


def carry(info, slots_at, use_at, states, decay):
    count, shape = len(states), states[0].shape
    return pl.pallas_call(
        functools.partial(carry_kernel, count, slots_at, use_at),
        in_specs=[SM] + [VM] * (count + 1),
        out_specs=[VM] * 2,
        out_shape=[jax.ShapeDtypeStruct((count // 2, *shape), f32)] * 2,
        scratch_shapes=[pltpu.VMEM((count, *shape), f32)] * 2,
        compiler_params=params(),
        name="carry_states",
    )(info, *states, decay)


def result_kernel(pairs, splits, here_at, info, *refs):
    refs = list(refs)
    take = lambda n: [refs.pop(0) for _ in range(n)]
    kept, arrived = take(len(pairs)), [take(n) for n in splits]
    carry_kept, carry_arrived, edge, *outs = refs
    eh, el = split2(edge[...])
    left = jnp.concatenate([eh, el, eh], axis=1)
    values = []
    for n, r in enumerate(pairs):
        ch, cl = split2(carry_kept[r] + carry_arrived[r])
        far = jnp.dot(left, jnp.concatenate([ch, ch, cl], axis=0), preferred_element_type=f32)
        other = jnp.concatenate([part[...] for part in arrived[n]], axis=0)
        values.append((kept[n][...] + other + far).astype(bf16))
    first = info[here_at] == 0
    outs[0][...] = jnp.where(first, values[0], values[1])
    outs[1][...] = jnp.where(first, values[1], values[0])


def results(info, here_at, pairs, kept, arrived, carries, edge):
    return pl.pallas_call(
        functools.partial(result_kernel, pairs, [len(parts) for parts in arrived], here_at),
        in_specs=[SM] + [VM] * (len(pairs) + sum(len(parts) for parts in arrived) + 3),
        out_specs=[VM] * len(pairs),
        out_shape=[jax.ShapeDtypeStruct(kept[0].shape, bf16)] * len(pairs),
        compiler_params=params(),
        name="finish_blocks",
    )(info, *kept, *[part for parts in arrived for part in parts], *carries, edge)


def arrange_kernel(count, lanes_at, info, *refs):
    out = refs[count]
    lanes = refs[0].shape[1]
    for r in range(count):
        out[:, pl.ds(pl.multiple_of(info[lanes_at + r] * lanes, lanes), lanes)] = refs[r][...]


def arrange(info, lanes_at, parts):
    rows, lanes = parts[0].shape
    return pl.pallas_call(
        functools.partial(arrange_kernel, len(parts), lanes_at),
        in_specs=[SM] + [VM] * len(parts),
        out_specs=VM,
        out_shape=jax.ShapeDtypeStruct((rows, lanes * len(parts)), bf16),
        compiler_params=params(),
        name="arrange_features",
    )(info, *parts)


def plain_tables(coeffs, rates, gains, width):
    lag = jnp.arange(width, dtype=f32)
    decay = jnp.exp(-rates[:, None] * lag[None, :])
    shift = lag[None, :] - lag[:, None]
    phi = jnp.dot(coeffs * gains[None, :], decay, precision=exact_prec)
    near = jnp.where(shift >= 0, phi[:, jnp.maximum(shift, 0).astype(jnp.int32)], 0.0)
    return jnp.concatenate([near, coeffs[:, :, None] * decay[None]], axis=1)


def plain_cut(mats, info, plan, half, cols):
    return [
        lax.dynamic_slice(mats, (lo, info[2 * i], info[2 * i + 1]), (n, half, cols)) for i, (lo, n) in enumerate(plan)
    ]


def plain_add(info, mine, other, mats, table, totals, work):
    results = []
    wide, width = mine[0].shape[1], table.shape[2]
    for b in range(len(mine)):
        rows = jnp.concatenate([mine[b], other[b]], axis=1)
        total = 0.0 if totals[b] is None else totals[b]
        for n in [n for n, at in work if at == b]:
            use = lax.dynamic_slice_in_dim(table, 2 * info[1 + n], mats[n].shape[0], 0)
            swapped = jnp.where(info[0] == 0, mats[n], jnp.roll(mats[n], wide, axis=2))
            proj = jnp.einsum("tj,kij->kti", rows, swapped, preferred_element_type=f32)
            proj = jnp.concatenate(jnp.split(proj, rows.shape[0] // width, axis=1), axis=2)
            total = total + jnp.einsum("kst,kti->si", use, proj, precision=exact_prec)
        results.append(total)
    return results


def plain_finish(info, totals, edge, decay, length):
    count, width = len(totals), edge.shape[0]
    subs = length // width
    held = jnp.zeros((count,) + totals[0].shape, f32)
    for s in range(count):
        held = lax.dynamic_update_slice(held, totals[s][None], (info[s], 0, 0))
    carried, values = jnp.zeros((edge.shape[1], totals[0].shape[1] // subs), f32), [None] * count
    for c in reversed(range(count)):
        enters = []
        for state in reversed(jnp.split(held[c, width:], subs, axis=1)):
            enters.append(carried)
            carried = state + decay * carried
        far = jnp.dot(edge, jnp.concatenate(enters[::-1], axis=1), precision=exact_prec)
        values[c] = jnp.concatenate(jnp.split(held[c, :width] + far, subs, axis=1), axis=0)
    values = jnp.stack(values)
    return [values[info[count + n]] for n in range(count)]


def plain_combine(parts):
    return sum(parts[1:], parts[0]).astype(bf16)


def plain_arrange(info, parts):
    rows, lanes = parts[0].shape
    out = jnp.zeros((rows, lanes * len(parts)), bf16)
    for r, part in enumerate(parts):
        out = lax.dynamic_update_slice(out, part, (0, info[r] * lanes))
    return out


def ring_of(count):
    order = [*range(0, count, 2), *reversed(range(1, count, 2))]
    offsets = [0]
    for step in range(1, count // 2):
        offsets += [-step, step]
    return order, [*offsets, count // 2]


def shift_of(x, ways, by_way, by_core):
    rank = lambda w, h: (w % ways) * 2 + h
    return lax.ppermute(x, "grp", [(rank(w, h), rank(w + by_way, h ^ by_core)) for w in range(ways) for h in range(2)])


def my_row(count, groups, numbers):
    rows = [numbers(c, g) for c in range(count) for g in range(groups)]
    ends = np.cumsum([len(part) for part in rows[0]])
    known = jnp.asarray(np.array([sum(r, []) for r in rows], np.int32))
    me = lax.axis_index("ctx") * groups + lax.axis_index("grp")
    row = lax.dynamic_slice(known, (me, 0), (1, known.shape[1]))[0]
    return row, [int(e) - len(part) for e, part in zip(ends, rows[0])], [int(e) for e in ends]


def plain_device(out_grad, filter_mats, coeffs, pole_rates):
    count, groups = lax.axis_size("ctx"), lax.axis_size("grp")
    ways, per_grp = groups // 2, count // groups
    per = count // ways
    own_filters, features, _ = filter_mats.shape
    length, wide = out_grad.shape
    half, width = features // 2, length // 4
    order, offsets = ring_of(count)
    right = [(order[i], order[(i + 1) % count]) for i in range(count)]
    left = [(b, a) for a, b in right]
    to = [(w, h) for w in range(1, ways) for h in range(2)] + [(0, 1), (0, 0)]
    plan = [(0, own_filters)] * len(to)

    def numbers(ctx, grp):
        way, here, at = grp // 2, grp % 2, order.index(ctx)
        cuts = []
        for w, h in to:
            cuts += [(here ^ h) * half, (way + w) % ways * 2 * wide]
        firsts = [(((way - w) % ways) * 2 + (here ^ h)) * (own_filters // 2) for w, h in to]
        turn = ctx % per_grp * 2 + here
        slots = [order[(at + o) % count] for o in offsets]
        use = [ways * ((r + turn) % per) + (way + w + ctx) % ways for w in range(ways) for r in range(per)]
        return [cuts, [here] + firsts, slots + use, [(ctx // ways - r) % per for r in range(per)]]

    row, begins, ends = my_row(count, groups, numbers)
    cuts, firsts, finish_info, lanes_info = [row[b:e] for b, e in zip(begins, ends)]
    swap = lambda x: shift_of(x, ways, 0, 1)
    mine, other = [out_grad], [swap(out_grad)]
    going_right, going_left = out_grad, out_grad
    for step in range(1, count // 2):
        going_right = lax.ppermute(going_right, "ctx", right)
        going_left = lax.ppermute(going_left, "ctx", left)
        mine += [going_right, going_left]
        other += [swap(going_right), swap(going_left)]
    mine.append(lax.ppermute(going_right, "ctx", right))
    other.append(swap(mine[-1]))
    pieces = plain_cut(filter_mats, cuts, plan, half, 2 * wide)
    mats = [shift_of(p, ways, w, h) for p, (w, h) in zip(pieces[:-1], to[:-1])] + pieces[-1:]
    gains = jnp.sqrt(-jnp.expm1(-2.0 * pole_rates))
    table = plain_tables(coeffs, pole_rates, gains, width)
    work = [(n, 0) for n in range(len(mats))]
    totals = [plain_add(firsts, [m], [o], mats, table, [None], work)[0] for m, o in zip(mine, other)]
    step_back = jnp.arange(width, dtype=f32) - width
    edge = gains[None, :] * jnp.exp(step_back[:, None] * pole_rates[None, :])
    decay = jnp.exp(-width * pole_rates)[:, None]
    partial = plain_finish(finish_info, totals, edge, decay, length)
    received = []
    for r in range(per):
        result = plain_combine([partial[r], *[shift_of(partial[w * per + r], ways, w, 0) for w in range(1, ways)]])
        pairs = []
        for c in range(count):
            for g in range(groups):
                m = (r + c % per_grp * 2 + g % 2) % per
                goal = ways * m + (g // 2 + c) % ways
                pairs.append((c * groups + g, goal * groups + c // per_grp))
        received.append(lax.ppermute(result, ("ctx", "grp"), pairs))
    return plain_arrange(lanes_info, received)


def spread(count, pairs, order, offsets):
    rand, best = random.Random(1), None

    def cost(flips):
        loads = {}
        for c in range(count):
            for r, pair in enumerate(pairs):
                for way in range(2):
                    goal = order[(order.index(c) + offsets[pair[way ^ flips[c][r]]]) % count]
                    lo, hi = sorted((c // 2, goal // 2))
                    keys = [(z, c % 2, way, goal > c) for z in range(lo, hi)]
                    if way != 2 * c // count:
                        keys.append((goal // 2, c % 2, way))
                    for key in keys:
                        loads[key] = loads.get(key, 0) + 1
        return max(loads.values()), sum(v * v for v in loads.values())

    for _ in range(20):
        flips = [[rand.randint(0, 1) for _ in pairs] for _ in range(count)]
        now, better = cost(flips), True
        while better:
            better = False
            for c in range(count):
                for r in range(len(pairs)):
                    flips[c][r] ^= 1
                    new = cost(flips)
                    if new < now:
                        now, better = new, True
                    else:
                        flips[c][r] ^= 1
        if best is None or now < best[0]:
            best = now, flips
    return best[1]


def final_rounds(count, groups):
    order, offsets = ring_of(count)
    if groups != 4 or count != 2 * groups:
        return None
    twos = [(s, s + 1) for s in range(1, count - 1, 2)] + [(0, count - 1)]
    pairs = twos[0::2] + twos[1::2]
    flips = spread(count, pairs, order, offsets)
    rounds = []
    for first in range(0, len(pairs), 2):
        for t in range(2):
            moves = []
            for c in range(count):
                for g in range(groups):
                    r = first + (t + g % 2) % 2
                    slot = pairs[r][g // 2 ^ flips[c][r]]
                    goal = order[(order.index(c) + offsets[slot]) % count]
                    moves.append((c * groups + g, goal * groups + c * groups // count))
            if len({b for _, b in moves}) != len(moves):
                return None
            rounds.append(moves)
    return pairs, flips, rounds


def per_device(out_grad, filter_mats, coeffs, pole_rates):
    count, groups = lax.axis_size("ctx"), lax.axis_size("grp")
    own_filters, features, _ = filter_mats.shape
    length, wide = out_grad.shape
    half, width = features // 2, length // 4
    tiled = half % 128 == 0 and wide % 128 == 0 and width % 128 == 0 and pole_rates.shape[0] % 16 == 0
    found = final_rounds(count, groups)
    if not tiled or own_filters % 4 or found is None:
        return plain_device(out_grad, filter_mats, coeffs, pole_rates)
    pairs, flips, rounds = found
    ways, per_grp = groups // 2, count // groups
    order, offsets = ring_of(count)
    right = [(order[i], order[(i + 1) % count]) for i in range(count)]
    left = [(b, a) for a, b in right]
    some = own_filters // 2
    far_to = [(1, h, 0, own_filters) for h in range(2)]
    swap_to = [(0, 1, lo, some) for lo in (0, some)]
    own_to = (0, 0, 0, own_filters)

    def numbers(ctx, grp):
        way, here, at = grp // 2, grp % 2, order.index(ctx)
        firsts = [(((way ^ w) * 2 + (here ^ h)) * own_filters + lo) // 2 for w, h, lo, _ in [*swap_to, own_to, *far_to]]
        slots = [order[(at + o) % count] for o in offsets]
        second = [way ^ flip for flip in flips[ctx]]
        use = [slots[p[t]] for p, t in zip(pairs, second)] + [slots[p[1 - t]] for p, t in zip(pairs, second)]
        senders = [next(a for a, b in moves if b == ctx * groups + grp) for moves in rounds]
        lanes = [a // groups % per_grp * 2 + a % 2 for a in senders]
        return [[here], second, firsts, slots, use, lanes]

    row, (core_at, second_at, firsts_at, slots_at, use_at, lanes_at), _ = my_row(count, groups, numbers)
    swap = lambda x: shift_of(x, ways, 0, 1)
    together = lambda *x: lax.optimization_barrier(x)

    pieces = cut(filter_mats, far_to[:1], half, 2 * wide)
    gains = jnp.sqrt(-jnp.expm1(-2.0 * pole_rates))
    table = ()
    cut_early = cut(filter_mats, [*swap_to, own_to, far_to[1]], half, 2 * wide)
    mats = [None, None, None, shift_of(pieces[0], ways, *far_to[0][:2])]
    going_right, going_left = out_grad, out_grad
    mine, other, totals = [out_grad], [swap(out_grad)], [None] * count
    back = lambda n: gains[None, :] * jnp.exp((jnp.arange(n, dtype=f32) - n)[:, None] * pole_rates[None, :])
    ahead = lambda n: jnp.exp(-n * pole_rates)[:, None]
    ends, far_ends = (back(width), ahead(width)), (back(length), ahead(length))

    done_sets, splits = {}, [1] * (len(pairs) - 1) + [2]

    def run(slots, use, closing=None):
        for s in slots:
            done_sets.setdefault(s, set()).update(use[s])
        chosen = sorted({n for s in slots for n in use[s]})
        info_at = [core_at] + [firsts_at + n for n in chosen]
        work = [(chosen.index(n), b) for n in chosen for b, s in enumerate(slots) if n in use[s]]
        got = add_blocks(
            row, info_at, [mine[s] for s in slots], [other[s] for s in slots], [mats[n] for n in chosen], table,
            [totals[s] for s in slots], work, *(() if closing is None else (ends, second_at + closing, splits[closing])),
        )
        if closing is not None:
            return got
        for s, t in zip(slots, got):
            totals[s] = t

    for step in range(1, count // 2 + 1):
        arrived = [0] if step == 1 else [2 * step - 3, 2 * step - 2]
        if step > 1:
            other += [swap(mine[s]) for s in arrived]
        if step < count // 2:
            coming = [lax.ppermute(going_right, "ctx", right), lax.ppermute(going_left, "ctx", left)]
        else:
            coming = [
                lax.ppermute(going_right[: length // 2], "ctx", right),
                lax.ppermute(going_left[length // 2 :], "ctx", left),
            ]
        if step == 3:
            piece, mats[3] = together(next_piece, mats[3])
            mats.append(shift_of(piece, ways, *far_to[1][:2]))
        if step == 2:
            table = tables(coeffs, later_rates, gains, width)
            mats[:2] = [swap(p) for p in pieces[:2]]
            mats[2], next_piece = pieces[2:]
        elif step > 2:
            slots = ([0] if step == 3 else []) + [2 * step - 5, 2 * step - 4]
            run(slots, {s: [0, 1, 2, 3] for s in slots})
        if step == count // 2:
            slots = [2 * step - 3, 2 * step - 2]
            run(slots, {s: [2] for s in slots})
        done = [s for s in range(count) if totals[s] is not None]
        coming, swapped, table, sums, early, filter_mats, cut_early = together(
            coming, other[-len(arrived) :], table, [totals[s] for s in done], mats[:4] if step > 1 else [], filter_mats, cut_early
        )
        if step == 1:
            pieces, row, coming = together(cut_early, row, coming)
        if step == 1:
            later_rates, coming = together(pole_rates, coming)
        other[-len(arrived) :] = swapped
        mats[: len(early)] = early
        for s, t in zip(done, sums):
            totals[s] = t
        if step < count // 2:
            going_right, going_left = coming
            mine += coming
        else:
            mine.append(jnp.concatenate(coming))
    other.append(swap(mine[-1]))

    kept, sent, states = [None] * len(pairs), [None] * len(pairs), [None] * count
    for pair in pairs:
        use = {s: [n for n in range(5) if n not in done_sets.get(s, ())] for s in pair}
        keep, *send = run(list(pair), use, pairs.index(pair))
        send, state = send[:-2], send[-2:]
        for s, st in zip(pair, state):
            states[s] = st
        kept[pairs.index(pair)], sent[pairs.index(pair)] = keep, send
    carry_kept, carry_sent = carry(row, slots_at, use_at, states, far_ends[1])
    carries = [carry_kept, shift_of(carry_sent, ways, 1, 0)]
    arrived = [[shift_of(x, ways, 1, 0) for x in parts] for parts in sent]
    received = []
    for first in range(0, len(pairs), 2):
        both = [first, first + 1]
        got = results(row, core_at, both, [kept[r] for r in both], [arrived[r] for r in both], carries, far_ends[0])
        received += [lax.ppermute(v, ("ctx", "grp"), moves) for v, moves in zip(got, rounds[first : first + 2])]
    return arrange(row, lanes_at, received)


def solution(mesh):
    placed = (P("ctx", "grp"), P("grp", "ctx", None), P(), P())
    return jax.shard_map(
        per_device, mesh=mesh, in_specs=placed, out_specs=P("ctx", "grp"), check_vma=False
    )
```

```python
import functools
import random

import jax
import jax.numpy as jnp
import numpy as np
from jax import lax
from jax.experimental import pallas as pl
from jax.experimental.pallas import tpu as pltpu
from jax.sharding import PartitionSpec as P

exact_prec = lax.Precision.HIGHEST
f32, bf16 = jnp.float32, jnp.bfloat16
NT = (((1,), (1,)), ((), ()))
VM = pl.BlockSpec(memory_space=pltpu.VMEM)
ANY = pl.BlockSpec(memory_space=pl.ANY)
SM = pl.BlockSpec(memory_space=pltpu.SMEM)


def params(mib=16):
    return pltpu.CompilerParams(vmem_limit_bytes=mib * 2**20)


def split2(x):
    high = x.astype(bf16)
    return high, (x - high.astype(f32)).astype(bf16)


def tables_kernel(poles_ref, out):
    poles, width = poles_ref.shape[0], out.shape[2] // 4
    rate, gain = poles_ref[:, 0:1], poles_ref[:, 1:2]
    lag = lax.broadcasted_iota(jnp.int32, (poles, width), 1).astype(f32)
    decay = jnp.exp(-rate * lag)
    gained = gain * decay
    columns = lax.broadcasted_iota(jnp.int32, (poles, poles_ref.shape[1]), 1)

    @pl.loop(0, out.shape[0])
    def _(pair):
        for j in range(2):
            chosen = jnp.where(columns == 2 + 2 * pair + j, poles_ref[...], 0.0)
            coef = jnp.sum(chosen, axis=1, keepdims=True)
            phi = jnp.sum(coef * gained, axis=0, keepdims=True)
            line = jnp.concatenate([phi, jnp.zeros((1, width), f32)], axis=1)
            rolled = pltpu.roll(jnp.broadcast_to(line, (width, 2 * width)), 0, 1, stride=1, stride_axis=0)
            near, weight = split2(rolled[:, :width]), split2(coef * decay)
            for at in range(2):
                lanes = slice((2 * at + j) * width, (2 * at + j + 1) * width)
                out[pair, :width, lanes] = near[at]
                out[pair, width:, lanes] = weight[at]


def tables(coeffs, rates, gains, width):
    filters, poles = coeffs.shape
    joined = jnp.concatenate([rates[:, None], gains[:, None], coeffs.T], axis=1)
    return pl.pallas_call(
        tables_kernel,
        in_specs=[VM],
        out_specs=VM,
        out_shape=jax.ShapeDtypeStruct((filters // 2, width + poles, 4 * width), bf16),
        compiler_params=params(),
        cost_estimate=pl.CostEstimate(flops=int(4e9), bytes_accessed=0, transcendentals=0),
        name="pole_tables",
    )(joined)


def cut_kernel(to, mats, *refs):
    outs, sems = refs[:-1], refs[-1]
    way, here = lax.axis_index("grp") // 2, lax.axis_index("grp") % 2
    copies = []
    for i, (by_way, by_core, lo, n) in enumerate(to):
        _, half, cols = outs[i].shape
        row = (1 - here if by_core else here) * half
        col = (1 - way if by_way else way) * cols
        src = mats.at[pl.ds(lo, n), pl.ds(pl.multiple_of(row, half), half), pl.ds(pl.multiple_of(col, cols), cols)]
        copies.append(pltpu.make_async_copy(src, outs[i], sems.at[i]))
    for c in copies:
        c.start()
    for c in copies:
        c.wait()


def cut(mats, to, half, cols):
    return pl.pallas_call(
        functools.partial(cut_kernel, to),
        in_specs=[ANY],
        out_specs=[VM] * len(to),
        out_shape=[jax.ShapeDtypeStruct((n, half, cols), bf16) for *_, n in to],
        scratch_shapes=[pltpu.SemaphoreType.DMA((len(to),))],
        compiler_params=params(60),
        name="cut_filters",
    )(mats)


def products(work, info_at, info, mine, other, mats, table, before, after, held):
    wide = mine[0].shape[1]
    here = info[info_at[0]]
    width = table.shape[2] // 4
    half = mats[0].shape[1]
    subs = mine[0].shape[0] // width
    units = [(i, n, b) for n, b in work for i in range(mats[n].shape[0] // 2)]
    for u, (i, n, b) in enumerate(units):
        two = mats[n].at[pl.ds(2 * i, 2)]
        m_mine = two[:, :, pl.ds(pl.multiple_of(here * wide, wide), wide)].reshape(2 * half, wide)
        m_other = two[:, :, pl.ds(pl.multiple_of((1 - here) * wide, wide), wide)].reshape(2 * half, wide)
        proj = lax.dot_general(mine[b][...], m_mine, NT, preferred_element_type=f32)
        proj += lax.dot_general(other[b][...], m_other, NT, preferred_element_type=f32)
        for at, part in enumerate(split2(proj)):
            for j in range(2):
                rows = pl.ds((2 * at + j) * width, width)
                for s in range(subs):
                    held[u, rows, s * half : (s + 1) * half] = part[
                        s * width : (s + 1) * width, j * half : (j + 1) * half
                    ]
    begun = set()
    for u, (i, n, b) in enumerate(units):
        pair = info[info_at[1 + n]] + i
        high, low = held[u, : 2 * width, :], held[u, 2 * width :, :]
        add = jnp.dot(table[pair, :, : 2 * width], high, preferred_element_type=f32)
        add += jnp.dot(table[pair, :, 2 * width :], high, preferred_element_type=f32)
        add += jnp.dot(table[pair, :, : 2 * width], low, preferred_element_type=f32)
        if b in begun:
            after[b][...] += add
        else:
            after[b][...] = add if before[b] is None else before[b][...] + add
            begun.add(b)


def blocks_kernel(blocks, sets, work, info_at, fresh, closing, splits, info, *refs):
    refs = list(refs)
    take = lambda n: [refs.pop(0) for _ in range(n)]
    mine, other, mats, (table,) = take(blocks), take(blocks), take(sets), take(1)
    before = [None if new else refs.pop(0) for new in fresh]
    if not closing:
        after, (held,) = take(blocks), take(1)
        products(work, info_at, info, mine, other, mats, table, before, after, held)
        return
    edge, decay, kept, *sent = take(3 + splits)
    states = take(blocks)
    held, after = refs
    after = [after.at[b] for b in range(blocks)]
    products(work, info_at, info, mine, other, mats, table, before, after, held)
    width, poles = edge.shape
    half = mats[0].shape[1]
    subs = mine[0].shape[0] // width
    eh, el = split2(edge[...])
    left = jnp.concatenate([eh, el, eh], axis=1)
    values = []
    for b in range(blocks):
        state, enters, carried = after[b][width:, :], [], jnp.zeros((poles, half), f32)
        for s in reversed(range(subs)):
            enters.append(carried)
            carried = state[:, s * half : (s + 1) * half] + decay[...] * carried
        states[b][...] = carried
        ch, cl = split2(jnp.concatenate(enters[::-1], axis=1))
        far = jnp.dot(left, jnp.concatenate([ch, ch, cl], axis=0), preferred_element_type=f32)
        values.append(after[b][:width, :] + far)
    first = info[closing] == 0
    rows = sent[0].shape[0]
    for s in range(subs):
        lanes, at = slice(s * half, (s + 1) * half), s * width
        one, two = [value[:, lanes] for value in values]
        kept[at : at + width, :] = jnp.where(first, one, two)
        sent[at // rows][at % rows : at % rows + width, :] = jnp.where(first, two, one)


def add_blocks(info, info_at, mine, other, mats, table, totals, work, ends=None, closing=0, splits=1):
    blocks, sets = len(mine), len(mats)
    fresh = [t is None for t in totals]
    old = [t for t in totals if t is not None]
    half, length = mats[0].shape[1], mine[0].shape[0]
    height, tw = table.shape[1:]
    lanes = length // (tw // 4) * half
    units = sum(mats[n].shape[0] // 2 for n, _ in work)
    first = 1 + 2 * blocks + sets + 1
    scratch = [pltpu.VMEM((units, tw, lanes), bf16)]
    if ends is None:
        ends, aliases = (), {first + i: b for i, b in enumerate(b for b in range(blocks) if not fresh[b])}
        shapes = [jax.ShapeDtypeStruct((height, lanes), f32)] * blocks
    else:
        aliases = {}
        shapes = [jax.ShapeDtypeStruct((length, half), f32)]
        shapes += [jax.ShapeDtypeStruct((length // splits, half), f32)] * splits
        shapes += [jax.ShapeDtypeStruct((height - tw // 4, half), f32)] * blocks
        scratch.append(pltpu.VMEM((blocks, height, lanes), f32))
    return pl.pallas_call(
        functools.partial(blocks_kernel, blocks, sets, work, info_at, fresh, closing, splits),
        in_specs=[SM] + [VM] * (2 * blocks + sets + 1 + len(old) + len(ends)),
        out_specs=[VM] * len(shapes),
        out_shape=shapes,
        scratch_shapes=scratch,
        input_output_aliases=aliases,
        compiler_params=params(14),
        cost_estimate=pl.CostEstimate(flops=int(units * 1.0e9), bytes_accessed=0, transcendentals=0),
        name="close_blocks" if closing else "add_blocks",
    )(info, *mine, *other, *mats, table, *old, *ends)


def carry_kernel(count, slots_at, use_at, info, *refs):
    states, decay, (kept, sent), (held, entering) = refs[:count], refs[count], refs[count + 1 : count + 3], refs[count + 3 :]
    for s in range(count):
        held[info[slots_at + s]] = states[s][...]
    carried = jnp.zeros_like(states[0])
    for c in reversed(range(count)):
        entering[c] = carried
        carried = held[c] + decay[...] * carried
    per = kept.shape[0]
    for r in range(per):
        kept[r] = entering[info[use_at + r]]
        sent[r] = entering[info[use_at + per + r]]


def carry(info, slots_at, use_at, states, decay):
    count, shape = len(states), states[0].shape
    return pl.pallas_call(
        functools.partial(carry_kernel, count, slots_at, use_at),
        in_specs=[SM] + [VM] * (count + 1),
        out_specs=[VM] * 2,
        out_shape=[jax.ShapeDtypeStruct((count // 2, *shape), f32)] * 2,
        scratch_shapes=[pltpu.VMEM((count, *shape), f32)] * 2,
        compiler_params=params(),
        name="carry_states",
    )(info, *states, decay)


def result_kernel(pairs, splits, here_at, info, *refs):
    refs = list(refs)
    take = lambda n: [refs.pop(0) for _ in range(n)]
    kept, arrived = take(len(pairs)), [take(n) for n in splits]
    carry_kept, carry_arrived, edge, *outs = refs
    eh, el = split2(edge[...])
    left = jnp.concatenate([eh, el, eh], axis=1)
    values = []
    for n, r in enumerate(pairs):
        ch, cl = split2(carry_kept[r] + carry_arrived[r])
        far = jnp.dot(left, jnp.concatenate([ch, ch, cl], axis=0), preferred_element_type=f32)
        other = jnp.concatenate([part[...] for part in arrived[n]], axis=0)
        values.append((kept[n][...] + other + far).astype(bf16))
    first = info[here_at] == 0
    outs[0][...] = jnp.where(first, values[0], values[1])
    outs[1][...] = jnp.where(first, values[1], values[0])


def results(info, here_at, pairs, kept, arrived, carries, edge):
    return pl.pallas_call(
        functools.partial(result_kernel, pairs, [len(parts) for parts in arrived], here_at),
        in_specs=[SM] + [VM] * (len(pairs) + sum(len(parts) for parts in arrived) + 3),
        out_specs=[VM] * len(pairs),
        out_shape=[jax.ShapeDtypeStruct(kept[0].shape, bf16)] * len(pairs),
        compiler_params=params(),
        name="finish_blocks",
    )(info, *kept, *[part for parts in arrived for part in parts], *carries, edge)


def arrange_kernel(count, lanes_at, info, *refs):
    out = refs[count]
    lanes = refs[0].shape[1]
    for r in range(count):
        out[:, pl.ds(pl.multiple_of(info[lanes_at + r] * lanes, lanes), lanes)] = refs[r][...]


def arrange(info, lanes_at, parts):
    rows, lanes = parts[0].shape
    return pl.pallas_call(
        functools.partial(arrange_kernel, len(parts), lanes_at),
        in_specs=[SM] + [VM] * len(parts),
        out_specs=VM,
        out_shape=jax.ShapeDtypeStruct((rows, lanes * len(parts)), bf16),
        compiler_params=params(),
        name="arrange_features",
    )(info, *parts)


def plain_tables(coeffs, rates, gains, width):
    lag = jnp.arange(width, dtype=f32)
    decay = jnp.exp(-rates[:, None] * lag[None, :])
    shift = lag[None, :] - lag[:, None]
    phi = jnp.dot(coeffs * gains[None, :], decay, precision=exact_prec)
    near = jnp.where(shift >= 0, phi[:, jnp.maximum(shift, 0).astype(jnp.int32)], 0.0)
    return jnp.concatenate([near, coeffs[:, :, None] * decay[None]], axis=1)


def plain_cut(mats, info, plan, half, cols):
    return [
        lax.dynamic_slice(mats, (lo, info[2 * i], info[2 * i + 1]), (n, half, cols)) for i, (lo, n) in enumerate(plan)
    ]


def plain_add(info, mine, other, mats, table, totals, work):
    results = []
    wide, width = mine[0].shape[1], table.shape[2]
    for b in range(len(mine)):
        rows = jnp.concatenate([mine[b], other[b]], axis=1)
        total = 0.0 if totals[b] is None else totals[b]
        for n in [n for n, at in work if at == b]:
            use = lax.dynamic_slice_in_dim(table, 2 * info[1 + n], mats[n].shape[0], 0)
            swapped = jnp.where(info[0] == 0, mats[n], jnp.roll(mats[n], wide, axis=2))
            proj = jnp.einsum("tj,kij->kti", rows, swapped, preferred_element_type=f32)
            proj = jnp.concatenate(jnp.split(proj, rows.shape[0] // width, axis=1), axis=2)
            total = total + jnp.einsum("kst,kti->si", use, proj, precision=exact_prec)
        results.append(total)
    return results


def plain_finish(info, totals, edge, decay, length):
    count, width = len(totals), edge.shape[0]
    subs = length // width
    held = jnp.zeros((count,) + totals[0].shape, f32)
    for s in range(count):
        held = lax.dynamic_update_slice(held, totals[s][None], (info[s], 0, 0))
    carried, values = jnp.zeros((edge.shape[1], totals[0].shape[1] // subs), f32), [None] * count
    for c in reversed(range(count)):
        enters = []
        for state in reversed(jnp.split(held[c, width:], subs, axis=1)):
            enters.append(carried)
            carried = state + decay * carried
        far = jnp.dot(edge, jnp.concatenate(enters[::-1], axis=1), precision=exact_prec)
        values[c] = jnp.concatenate(jnp.split(held[c, :width] + far, subs, axis=1), axis=0)
    values = jnp.stack(values)
    return [values[info[count + n]] for n in range(count)]


def plain_combine(parts):
    return sum(parts[1:], parts[0]).astype(bf16)


def plain_arrange(info, parts):
    rows, lanes = parts[0].shape
    out = jnp.zeros((rows, lanes * len(parts)), bf16)
    for r, part in enumerate(parts):
        out = lax.dynamic_update_slice(out, part, (0, info[r] * lanes))
    return out


def ring_of(count):
    order = [*range(0, count, 2), *reversed(range(1, count, 2))]
    offsets = [0]
    for step in range(1, count // 2):
        offsets += [-step, step]
    return order, [*offsets, count // 2]


def shift_of(x, ways, by_way, by_core):
    rank = lambda w, h: (w % ways) * 2 + h
    return lax.ppermute(x, "grp", [(rank(w, h), rank(w + by_way, h ^ by_core)) for w in range(ways) for h in range(2)])


def my_row(count, groups, numbers):
    rows = [numbers(c, g) for c in range(count) for g in range(groups)]
    ends = np.cumsum([len(part) for part in rows[0]])
    known = jnp.asarray(np.array([sum(r, []) for r in rows], np.int32))
    me = lax.axis_index("ctx") * groups + lax.axis_index("grp")
    row = lax.dynamic_slice(known, (me, 0), (1, known.shape[1]))[0]
    return row, [int(e) - len(part) for e, part in zip(ends, rows[0])], [int(e) for e in ends]


def plain_device(out_grad, filter_mats, coeffs, pole_rates):
    count, groups = lax.axis_size("ctx"), lax.axis_size("grp")
    ways, per_grp = groups // 2, count // groups
    per = count // ways
    own_filters, features, _ = filter_mats.shape
    length, wide = out_grad.shape
    half, width = features // 2, length // 4
    order, offsets = ring_of(count)
    right = [(order[i], order[(i + 1) % count]) for i in range(count)]
    left = [(b, a) for a, b in right]
    to = [(w, h) for w in range(1, ways) for h in range(2)] + [(0, 1), (0, 0)]
    plan = [(0, own_filters)] * len(to)

    def numbers(ctx, grp):
        way, here, at = grp // 2, grp % 2, order.index(ctx)
        cuts = []
        for w, h in to:
            cuts += [(here ^ h) * half, (way + w) % ways * 2 * wide]
        firsts = [(((way - w) % ways) * 2 + (here ^ h)) * (own_filters // 2) for w, h in to]
        turn = ctx % per_grp * 2 + here
        slots = [order[(at + o) % count] for o in offsets]
        use = [ways * ((r + turn) % per) + (way + w + ctx) % ways for w in range(ways) for r in range(per)]
        return [cuts, [here] + firsts, slots + use, [(ctx // ways - r) % per for r in range(per)]]

    row, begins, ends = my_row(count, groups, numbers)
    cuts, firsts, finish_info, lanes_info = [row[b:e] for b, e in zip(begins, ends)]
    swap = lambda x: shift_of(x, ways, 0, 1)
    mine, other = [out_grad], [swap(out_grad)]
    going_right, going_left = out_grad, out_grad
    for step in range(1, count // 2):
        going_right = lax.ppermute(going_right, "ctx", right)
        going_left = lax.ppermute(going_left, "ctx", left)
        mine += [going_right, going_left]
        other += [swap(going_right), swap(going_left)]
    mine.append(lax.ppermute(going_right, "ctx", right))
    other.append(swap(mine[-1]))
    pieces = plain_cut(filter_mats, cuts, plan, half, 2 * wide)
    mats = [shift_of(p, ways, w, h) for p, (w, h) in zip(pieces[:-1], to[:-1])] + pieces[-1:]
    gains = jnp.sqrt(-jnp.expm1(-2.0 * pole_rates))
    table = plain_tables(coeffs, pole_rates, gains, width)
    work = [(n, 0) for n in range(len(mats))]
    totals = [plain_add(firsts, [m], [o], mats, table, [None], work)[0] for m, o in zip(mine, other)]
    step_back = jnp.arange(width, dtype=f32) - width
    edge = gains[None, :] * jnp.exp(step_back[:, None] * pole_rates[None, :])
    decay = jnp.exp(-width * pole_rates)[:, None]
    partial = plain_finish(finish_info, totals, edge, decay, length)
    received = []
    for r in range(per):
        result = plain_combine([partial[r], *[shift_of(partial[w * per + r], ways, w, 0) for w in range(1, ways)]])
        pairs = []
        for c in range(count):
            for g in range(groups):
                m = (r + c % per_grp * 2 + g % 2) % per
                goal = ways * m + (g // 2 + c) % ways
                pairs.append((c * groups + g, goal * groups + c // per_grp))
        received.append(lax.ppermute(result, ("ctx", "grp"), pairs))
    return plain_arrange(lanes_info, received)


def spread(count, pairs, order, offsets):
    rand, best = random.Random(1), None

    def cost(flips):
        loads = {}
        for c in range(count):
            for r, pair in enumerate(pairs):
                for way in range(2):
                    goal = order[(order.index(c) + offsets[pair[way ^ flips[c][r]]]) % count]
                    lo, hi = sorted((c // 2, goal // 2))
                    keys = [(z, c % 2, way, goal > c) for z in range(lo, hi)]
                    if way != 2 * c // count:
                        keys.append((goal // 2, c % 2, way))
                    for key in keys:
                        loads[key] = loads.get(key, 0) + 1
        return max(loads.values()), sum(v * v for v in loads.values())

    for _ in range(20):
        flips = [[rand.randint(0, 1) for _ in pairs] for _ in range(count)]
        now, better = cost(flips), True
        while better:
            better = False
            for c in range(count):
                for r in range(len(pairs)):
                    flips[c][r] ^= 1
                    new = cost(flips)
                    if new < now:
                        now, better = new, True
                    else:
                        flips[c][r] ^= 1
        if best is None or now < best[0]:
            best = now, flips
    return best[1]


def final_rounds(count, groups):
    order, offsets = ring_of(count)
    if groups != 4 or count != 2 * groups:
        return None
    twos = [(s, s + 1) for s in range(1, count - 1, 2)] + [(0, count - 1)]
    pairs = twos[0::2] + twos[1::2]
    flips = spread(count, pairs, order, offsets)
    rounds = []
    for first in range(0, len(pairs), 2):
        for t in range(2):
            moves = []
            for c in range(count):
                for g in range(groups):
                    r = first + (t + g % 2) % 2
                    slot = pairs[r][g // 2 ^ flips[c][r]]
                    goal = order[(order.index(c) + offsets[slot]) % count]
                    moves.append((c * groups + g, goal * groups + c * groups // count))
            if len({b for _, b in moves}) != len(moves):
                return None
            rounds.append(moves)
    return pairs, flips, rounds


def per_device(out_grad, filter_mats, coeffs, pole_rates):
    count, groups = lax.axis_size("ctx"), lax.axis_size("grp")
    own_filters, features, _ = filter_mats.shape
    length, wide = out_grad.shape
    half, width = features // 2, length // 4
    tiled = half % 128 == 0 and wide % 128 == 0 and width % 128 == 0 and pole_rates.shape[0] % 16 == 0
    found = final_rounds(count, groups)
    if not tiled or own_filters % 4 or found is None:
        return plain_device(out_grad, filter_mats, coeffs, pole_rates)
    pairs, flips, rounds = found
    ways, per_grp = groups // 2, count // groups
    order, offsets = ring_of(count)
    right = [(order[i], order[(i + 1) % count]) for i in range(count)]
    left = [(b, a) for a, b in right]
    some = own_filters // 2
    far_to = [(1, h, 0, own_filters) for h in range(2)]
    swap_to = [(0, 1, lo, some) for lo in (0, some)]
    own_to = (0, 0, 0, own_filters)

    def numbers(ctx, grp):
        way, here, at = grp // 2, grp % 2, order.index(ctx)
        firsts = [(((way ^ w) * 2 + (here ^ h)) * own_filters + lo) // 2 for w, h, lo, _ in [*swap_to, own_to, *far_to]]
        slots = [order[(at + o) % count] for o in offsets]
        second = [way ^ flip for flip in flips[ctx]]
        use = [slots[p[t]] for p, t in zip(pairs, second)] + [slots[p[1 - t]] for p, t in zip(pairs, second)]
        senders = [next(a for a, b in moves if b == ctx * groups + grp) for moves in rounds]
        lanes = [a // groups % per_grp * 2 + a % 2 for a in senders]
        return [[here], second, firsts, slots, use, lanes]

    row, (core_at, second_at, firsts_at, slots_at, use_at, lanes_at), _ = my_row(count, groups, numbers)
    swap = lambda x: shift_of(x, ways, 0, 1)
    together = lambda *x: lax.optimization_barrier(x)

    pieces = cut(filter_mats, far_to[:1], half, 2 * wide)
    gains = jnp.sqrt(-jnp.expm1(-2.0 * pole_rates))
    table = ()
    cut_early = cut(filter_mats, [*swap_to, own_to, far_to[1]], half, 2 * wide)
    mats = [None, None, None, shift_of(pieces[0], ways, *far_to[0][:2])]
    going_right, going_left = out_grad, out_grad
    mine, other, totals = [out_grad], [swap(out_grad)], [None] * count
    back = lambda n: gains[None, :] * jnp.exp((jnp.arange(n, dtype=f32) - n)[:, None] * pole_rates[None, :])
    ahead = lambda n: jnp.exp(-n * pole_rates)[:, None]
    ends, far_ends = (back(width), ahead(width)), (back(length), ahead(length))

    done_sets, splits = {}, [1] * (len(pairs) - 1) + [2]

    def run(slots, use, closing=None):
        for s in slots:
            done_sets.setdefault(s, set()).update(use[s])
        chosen = sorted({n for s in slots for n in use[s]})
        info_at = [core_at] + [firsts_at + n for n in chosen]
        work = [(chosen.index(n), b) for n in chosen for b, s in enumerate(slots) if n in use[s]]
        got = add_blocks(
            row, info_at, [mine[s] for s in slots], [other[s] for s in slots], [mats[n] for n in chosen], table,
            [totals[s] for s in slots], work, *(() if closing is None else (ends, second_at + closing, splits[closing])),
        )
        if closing is not None:
            return got
        for s, t in zip(slots, got):
            totals[s] = t

    for step in range(1, count // 2 + 1):
        arrived = [0] if step == 1 else [2 * step - 3, 2 * step - 2]
        if step > 1:
            other += [swap(mine[s]) for s in arrived]
        if step < count // 2:
            coming = [lax.ppermute(going_right, "ctx", right), lax.ppermute(going_left, "ctx", left)]
        else:
            coming = [
                lax.ppermute(going_right[: length // 2], "ctx", right),
                lax.ppermute(going_left[length // 2 :], "ctx", left),
            ]
        if step == 3:
            piece, mats[3] = together(next_piece, mats[3])
            mats.append(shift_of(piece, ways, *far_to[1][:2]))
        if step == 2:
            table = tables(coeffs, later_rates, gains, width)
            mats[:2] = [swap(p) for p in pieces[:2]]
            mats[2], next_piece = pieces[2:]
        elif step > 2:
            slots = ([0] if step == 3 else []) + [2 * step - 5, 2 * step - 4]
            run(slots, {s: [0, 1, 2, 3] for s in slots})
        if step == count // 2:
            slots = [2 * step - 3, 2 * step - 2]
            run(slots, {s: [2] for s in slots})
        done = [s for s in range(count) if totals[s] is not None]
        coming, swapped, table, sums, early, filter_mats, cut_early = together(
            coming, other[-len(arrived) :], table, [totals[s] for s in done], mats[:4] if step > 1 else [], filter_mats, cut_early
        )
        if step == 1:
            pieces, row, coming = together(cut_early, row, coming)
        if step == 1:
            later_rates, coming = together(pole_rates, coming)
        other[-len(arrived) :] = swapped
        mats[: len(early)] = early
        for s, t in zip(done, sums):
            totals[s] = t
        if step < count // 2:
            going_right, going_left = coming
            mine += coming
        else:
            mine.append(jnp.concatenate(coming))
    other.append(swap(mine[-1]))

    kept, sent, states = [None] * len(pairs), [None] * len(pairs), [None] * count
    for pair in pairs:
        use = {s: [n for n in range(5) if n not in done_sets.get(s, ())] for s in pair}
        keep, *send = run(list(pair), use, pairs.index(pair))
        send, state = send[:-2], send[-2:]
        for s, st in zip(pair, state):
            states[s] = st
        kept[pairs.index(pair)], sent[pairs.index(pair)] = keep, send
    carry_kept, carry_sent = carry(row, slots_at, use_at, states, far_ends[1])
    carries = [carry_kept, shift_of(carry_sent, ways, 1, 0)]
    arrived = [[shift_of(x, ways, 1, 0) for x in parts] for parts in sent]
    received = []
    for first in range(0, len(pairs), 2):
        both = [first, first + 1]
        got = results(row, core_at, both, [kept[r] for r in both], [arrived[r] for r in both], carries, far_ends[0])
        received += [lax.ppermute(v, ("ctx", "grp"), moves) for v, moves in zip(got, rounds[first : first + 2])]
    return arrange(row, lanes_at, received)


def solution(mesh):
    placed = (P("ctx", "grp"), P("grp", "ctx", None), P(), P())
    return jax.shard_map(
        per_device, mesh=mesh, in_specs=placed, out_specs=P("ctx", "grp"), check_vma=False
    )
```
